512 devices in a mesh: dp: 32 (over x_lo, z), seq: 16 (over x_hi, y, core).
Axes of the slice: x: 4 (x_hi: 2, x_lo: 2; x = x_hi * 2 + x_lo), y: 4, z: 16, core: 2. Of those that a mesh axis runs over, the one named last changes fastest.
Arguments:
- q_raw: bfloat16 [32, 2048, 2048], P('dp', 'seq'), may hold values from -6 to 6
- key_unnormed: bfloat16 [32, 2048, 1024], P('dp', 'seq'), may hold values from -6 to 6
- value_input: bfloat16 [32, 2048, 1024], P('dp', 'seq'), may hold values from -24 to 24
- grad_attended: bfloat16 [32, 2048, 2048], P('dp', 'seq'), may hold values from -48 to 48
- segment_ids: int32 [32, 2048], P('dp', 'seq'), may hold values from 0 to 3, never falling along the last dimension, each value on 1 to 1024 neighbouring positions
- q_gain: float32 [128], replicated, may hold values from 0.1 to 1.9
- key_norm_gain: float32 [128], replicated, may hold values from 0.1 to 1.9
Outputs:
- attended: bfloat16 [32, 2048, 2048], P('dp', 'seq')
- grad_q: bfloat16 [32, 2048, 2048], P('dp', 'seq')
- grad_k: bfloat16 [32, 2048, 1024], P('dp', 'seq')
- grad_value: bfloat16 [32, 2048, 1024], P('dp', 'seq')
- grad_q_gain: float32 [128], replicated
- key_gain_gradient: float32 [128], replicated
The draws below stay inside these ranges and needn't reach their ends.
Inputs may be any that keep to these rules, and one draw needn't show every extreme that they name: `segment_ids`: within a trajectory the numbers never fall; every document number appears, a document holds at most 1024 tokens, and one holds exactly that many.
All inputs are finite; a program needn't handle non-finite values.
Results may differ from the reference program's by a relative error of at most 0.0085.
Values may be sent and summed in bfloat16 or wider, within the bound.
A program may use at most 64 MiB of HBM per device.

```python
import math
import jax
import jax.numpy as jnp
import numpy as np
from jax import lax

HEAD_SIZE = 128
QUERY_HEADS = 16
KEY_VALUE_HEADS = 8
SEGS = 4
TRAJECTORY_LEN = 2048
TRAJECTORY_COUNT = 32


def steps_of(key, extent, cuts, smallest, largest):
    loudness, own = 1.0, jax.random.fold_in(key, 6)
    for axis_at, shards_of in cuts:
        draws = jnp.exp(jax.random.uniform(jax.random.fold_in(own, axis_at), (shards_of,), jnp.float32, smallest / len(cuts), largest / len(cuts)))
        loudness = loudness * jnp.repeat(draws, extent[axis_at] // shards_of).reshape([-1 if axis == axis_at else 1 for axis in range(len(extent))])
    return loudness


def profile(count, total, bound, lean):
    portions = [(1 << 20) // math.isqrt(rank ** lean) + 1 for rank in range(2, count + 1)]
    spare, holding = total - bound - (count - 1), [1] * (count - 1)
    while spare > 0:
        movable = [i for i in range(count - 1) if holding[i] < bound]
        whole, remaining = sum([portions[i] for i in movable]), spare
        for i in movable:
            addition = min(bound - holding[i], max(1, remaining * portions[i] // whole), spare)
            holding[i] = holding[i] + addition
            spare = spare - addition
    return np.array([bound] + holding)


def ragged(stream_key, amount, total, limit, slope):
    if amount == 2:
        one = jax.random.randint(stream_key, (), max(1, total - limit), min(limit, total - 1) + 1)
        return jnp.stack([one, total - one])
    lengths = jnp.asarray(profile(amount, total, limit, slope), jnp.int32)
    twos = (amount - 1) // 2
    donor, sink = lengths[1:1 + 2 * twos:2], lengths[2:2 + 2 * twos:2]
    margin = jnp.minimum(donor - 1, limit - sink)
    shifted = jax.random.randint(jax.random.fold_in(stream_key, 1), (twos,), 0, 1 << 20) % (margin + 1)
    lengths = lengths.at[1:1 + 2 * twos:2].set(donor - shifted).at[2:2 + 2 * twos:2].set(sink + shifted)
    return lengths[jax.random.permutation(jax.random.fold_in(stream_key, 2), amount)]


def bell_draw(rng, extent, spread, bound, shards=(), kind=jnp.bfloat16):
    array = jax.random.normal(rng, extent, jnp.float32) * spread
    if len(shards) > 0:
        array = steps_of(rng, extent, shards, -0.22, 0.18) * array
    return jnp.clip(array, min=-bound, max=bound).astype(kind)


def setup_inputs(seed: int = 0) -> dict:
    streams_of = jax.random.split(jax.random.key(seed), 8)
    return {
        "q_raw": bell_draw(streams_of[0], (TRAJECTORY_COUNT, TRAJECTORY_LEN, QUERY_HEADS * HEAD_SIZE), 1.0, 6.0, ((0, 32), (1, 16))),
        "key_unnormed": bell_draw(streams_of[1], (TRAJECTORY_COUNT, TRAJECTORY_LEN, KEY_VALUE_HEADS * HEAD_SIZE), 1.0, 6.0, ((0, 32), (1, 16))),
        "value_input": bell_draw(streams_of[2], (TRAJECTORY_COUNT, TRAJECTORY_LEN, KEY_VALUE_HEADS * HEAD_SIZE), 4.0, 24.0, ((0, 32), (1, 16))),
        "grad_attended": bell_draw(streams_of[3], (TRAJECTORY_COUNT, TRAJECTORY_LEN, QUERY_HEADS * HEAD_SIZE), 8.0, 48.0, ((0, 32), (1, 16))),
        "segment_ids": jax.vmap(lambda own: jnp.searchsorted(jnp.cumsum(ragged(own, SEGS, TRAJECTORY_LEN, TRAJECTORY_LEN // 2, 0)), jnp.arange(TRAJECTORY_LEN), side="right"))(jax.random.split(streams_of[4], TRAJECTORY_COUNT)).reshape((TRAJECTORY_COUNT, TRAJECTORY_LEN)).astype(jnp.int32),
        "q_gain": jnp.clip(1.0 + 0.18 * jax.random.normal(streams_of[5], (HEAD_SIZE,), jnp.float32), 0.1, 1.9),
        "key_norm_gain": jnp.clip(1.0 + 0.18 * jax.random.normal(streams_of[6], (HEAD_SIZE,), jnp.float32), 0.1, 1.9),
    }


EPSILON = 1e-06

def unit_components(vectors, gain_vec):
    vectors = vectors.astype(jnp.float32)
    inverse = lax.rsqrt(lax.optimization_barrier(jnp.mean(vectors * vectors, axis=-1, keepdims=True)) + EPSILON)
    unit_rows = vectors * inverse
    return (inverse, unit_rows, (unit_rows * gain_vec).astype(jnp.bfloat16))

def norm_backward_pass(gradient, inverse, unit_rows, gain_vec):
    scaled = gradient * gain_vec
    centred = scaled - unit_rows * lax.optimization_barrier(jnp.mean(scaled * unit_rows, axis=-1, keepdims=True))
    return (inverse * centred).astype(jnp.bfloat16)

def one_head(q_head, k_head, v_head, g_head, allowed):
    score_scale = q_head.shape[-1] ** (-0.5)
    scores = jnp.dot(q_head, k_head.T, preferred_element_type=jnp.float32) * score_scale
    exp_scores = jnp.where(allowed, jnp.exp(scores), 0.0)
    weights = exp_scores / lax.optimization_barrier(jnp.sum(exp_scores, axis=-1, keepdims=True))
    weights_b = weights.astype(jnp.bfloat16)
    attended = jnp.dot(weights_b, v_head, preferred_element_type=jnp.float32).astype(jnp.bfloat16)
    grad_weights = jnp.dot(g_head, v_head.T, preferred_element_type=jnp.float32)
    row_term = lax.optimization_barrier(jnp.sum(weights * grad_weights, axis=-1, keepdims=True))
    grad_scores = (weights * (grad_weights - row_term) * score_scale).astype(jnp.bfloat16)
    grad_query = jnp.dot(grad_scores, k_head, preferred_element_type=jnp.float32)
    key_gradient = jnp.dot(grad_scores.T, q_head, preferred_element_type=jnp.float32)
    value_gradient = jnp.dot(weights_b.T, g_head, preferred_element_type=jnp.float32)
    return (attended, grad_query, key_gradient, value_gradient)

def reference(q_raw, key_unnormed, value_input, grad_attended, segment_ids, q_gain, key_norm_gain):
    group_width = QUERY_HEADS // KEY_VALUE_HEADS

    def one_sequence(inputs):
        q_seq, key_sequence, value_sequence, gradient_sequence, segment = inputs
        sequence_length = q_seq.shape[0]
        q_inv, q_unit, query_gain_scaled = unit_components(q_seq.reshape(sequence_length, QUERY_HEADS, HEAD_SIZE), q_gain)
        key_inverse_norm, key_unit_length, key_gain_scaled = unit_components(key_sequence.reshape(sequence_length, KEY_VALUE_HEADS, HEAD_SIZE), key_norm_gain)
        positions = jnp.arange(sequence_length, dtype=jnp.int32)
        allowed = (positions[None, :] <= positions[:, None]) & (segment[None, :] == segment[:, None])
        query_groups = query_gain_scaled.reshape(sequence_length, KEY_VALUE_HEADS, group_width, HEAD_SIZE).transpose(1, 2, 0, 3)
        gradient_query_groups = gradient_sequence.reshape(sequence_length, KEY_VALUE_HEADS, group_width, HEAD_SIZE).transpose(1, 2, 0, 3)
        k_heads = key_gain_scaled.transpose(1, 0, 2)
        value_head_list = value_sequence.reshape(sequence_length, KEY_VALUE_HEADS, HEAD_SIZE).transpose(1, 0, 2)

        def per_key_head(head_inputs):
            k_head, v_head, q_group, g_group = head_inputs
            results = [one_head(q_group[member], k_head, v_head, g_group[member], allowed) for member in range(group_width)]
            attended = jnp.stack([item[0] for item in results])
            grad_query = jnp.stack([item[1] for item in results])
            key_gradient = results[0][2]
            value_gradient = results[0][3]
            for item in results[1:]:
                key_gradient = key_gradient + item[2]
                value_gradient = value_gradient + item[3]
            return (attended, grad_query, key_gradient, value_gradient.astype(jnp.bfloat16))
        attended, grad_query, key_gradient, value_gradient = lax.map(per_key_head, (k_heads, value_head_list, query_groups, gradient_query_groups))
        attended = attended.transpose(2, 0, 1, 3).reshape(sequence_length, QUERY_HEADS * HEAD_SIZE)
        grad_query = grad_query.transpose(2, 0, 1, 3).reshape(sequence_length, QUERY_HEADS, HEAD_SIZE)
        key_gradient = key_gradient.transpose(1, 0, 2)
        value_gradient = value_gradient.transpose(1, 0, 2).reshape(sequence_length, KEY_VALUE_HEADS * HEAD_SIZE)
        out_q = norm_backward_pass(grad_query, q_inv, q_unit, q_gain).reshape(sequence_length, QUERY_HEADS * HEAD_SIZE)
        output_key = norm_backward_pass(key_gradient, key_inverse_norm, key_unit_length, key_norm_gain).reshape(sequence_length, KEY_VALUE_HEADS * HEAD_SIZE)
        part_q = lax.optimization_barrier(jnp.sum(grad_query * q_unit, axis=(0, 1)))
        key_portion = lax.optimization_barrier(jnp.sum(key_gradient * key_unit_length, axis=(0, 1)))
        return (attended, out_q, output_key, value_gradient, part_q, key_portion)
    attended, out_q, output_key, value_gradient, part_q, key_portion = lax.map(one_sequence, (q_raw, key_unnormed, value_input, grad_attended, segment_ids))
    grad_q_gain = lax.optimization_barrier(jnp.sum(part_q, axis=0)) / math.sqrt(TRAJECTORY_COUNT * TRAJECTORY_LEN * QUERY_HEADS)
    key_gain_gradient = lax.optimization_barrier(jnp.sum(key_portion, axis=0)) / math.sqrt(TRAJECTORY_COUNT * TRAJECTORY_LEN * KEY_VALUE_HEADS)
    return (attended, out_q, output_key, value_gradient, grad_q_gain, key_gain_gradient)
```

```python
import functools
import math

import jax
import jax.numpy as jnp
from jax import lax
from jax.experimental import pallas as pl
from jax.experimental.pallas import tpu as pltpu
from jax.sharding import PartitionSpec as P

MESH = pl.DeviceIdType.MESH
EPSILON = 1e-06
D = 128
TOK = 128
SEQ = 16
HEADS_KV = 8
LEN = TOK * SEQ
B = 256
NB = LEN // B
BAND = 5
PAD = LEN + B
ONES = 16
FAR = -16384.0
F32, BF16 = jnp.float32, jnp.bfloat16
NT = (((1,), (1,)), ((), ()))


def _rows(start, count):
    return pl.ds(pl.multiple_of(start, count), count)


def _dot(a, b):
    return jnp.dot(a, b, preferred_element_type=F32)


def _inverse_norm(x):
    return lax.rsqrt(jnp.mean(x * x, axis=-1, keepdims=True) + EPSILON)


def _norm_backward(grad, inverse, unit, gain):
    scaled = grad * gain
    return inverse * (scaled - unit * jnp.mean(scaled * unit, axis=-1, keepdims=True))


def _fold(x):
    return jnp.sum(x.reshape(x.shape[0] // 8, 8, D), axis=0)


def _grouped(body):
    for first, last, blocks in ((0, 4, BAND), (4, 6, 4), (6, 8, 2)):
        lax.fori_loop(first, last, lambda j, _, blocks=blocks: (body(j, blocks), 0)[1], 0)


def kernel(
    q_in, k_in, v_in, g_in, seg_in, qg_in, kg_in,
    o_out, dq_out, dk_out, dv_out, gain_out,
    q_buf, k_buf, v_aug, g_aug, seg_buf, q_aug, k_aug, k_t, v_t, e_buf,
    o_acc, o32, o_bf, inv_col, inv_row, g_inv, q_inv, dq_acc, dk_buf, dv_buf, x_k, x_v,
    gq_bf, gk_bf, gv_bf, part, gain_src, gain_seq, z_src, z_four, zq_src, z_all,
    ss, rs, rs_k, rs_v, rs_xk, rs_xv,
):
    dp, me = lax.axis_index("dp"), lax.axis_index("seq")
    chip, core = me // 2, me % 2
    sib = me + 1 - 2 * core
    x_lo, z = dp // 16, dp % 16
    score_scale = D ** (-0.5)
    exponent_scale = score_scale * math.log2(math.e)

    (S_SEG, S_K, S_Q, S_V, S_G, S_KF, S_VF, S_O, S_DQ, S_XK, S_XV, S_DK, S_DV, S_GAIN, S_Z4, S_Z4B, S_ZA, S_Z5) = range(18)

    def at_seq(i):
        return (dp, i)

    def at_z(dx, dz):
        return (((x_lo + dx) % 2) * 16 + (z + dz + 16) % 16, me)

    z_peers = [at_z(0, 4), at_z(0, -4), at_z(0, 1), at_z(0, -1), at_z(0, 2), at_z(0, -2)]
    z_peers += [at_z(1, 0), at_z(1, 1), at_z(1, -1), at_z(1, 2), at_z(1, -2)]

    barrier = pltpu.get_barrier_semaphore()

    def greet(k, _):
        pl.semaphore_signal(barrier, inc=1, device_id=at_seq((me + k) % SEQ), device_id_type=MESH)
        return 0

    lax.fori_loop(1, SEQ, greet, 0)
    for peer in z_peers:
        pl.semaphore_signal(barrier, inc=1, device_id=peer, device_id_type=MESH)

    zero_block = jnp.zeros((B, D), F32)
    lane = lax.broadcasted_iota(jnp.int32, (D, D), 1)
    v_aug[:, D:] = jnp.ones((LEN, D), BF16)
    v_t[D:, :] = jnp.ones((ONES, LEN), BF16)
    o_acc[...] = jnp.zeros_like(o_acc)
    dq_acc[...] = jnp.zeros_like(dq_acc)
    part[...] = jnp.zeros_like(part)
    q_aug[LEN:, :D] = zero_block.astype(BF16)
    q_aug[LEN:, D:] = jnp.ones((B, D), BF16)
    g_aug[LEN:, :] = jnp.zeros((B, 2 * D), BF16)
    g_inv[LEN:, :] = zero_block.astype(BF16)
    q_inv[LEN:, :] = zero_block.astype(BF16)

    pl.semaphore_wait(barrier, SEQ - 1 + len(z_peers))

    def remote(src, dst, send, recv, peer):
        pltpu.make_async_remote_copy(src_ref=src, dst_ref=dst, send_sem=send, recv_sem=recv, device_id=peer, device_id_type=MESH).start()

    def local(src, dst, sem):
        pltpu.make_async_copy(src, dst, sem).start()

    def drain(ref, sem):
        pltpu.make_async_copy(ref, ref, sem).wait()

    mine = _rows(me * TOK, TOK)

    def send_seg(k, _):
        remote(seg_in, seg_buf.at[pl.ds(me, 1)], ss.at[S_SEG], rs.at[S_SEG], at_seq((me + k) % SEQ))
        return 0

    local(seg_in, seg_buf.at[pl.ds(me, 1)], rs.at[S_SEG])
    lax.fori_loop(1, SEQ, send_seg, 0)

    def send_heads(src, dst, s):
        local(src.at[0, :, _rows(me * D, D)], dst, rs.at[s])

        def one(k, _):
            to = (me + k) % SEQ
            remote(src.at[0, :, _rows(to * D, D)], dst, ss.at[s], rs.at[s], at_seq(to))
            return 0

        lax.fori_loop(1, SEQ, one, 0)

    def send_key_heads(src, dst, s, sems):
        local(src.at[0, :, _rows(chip * D, D)], dst, sems.at[chip])

        def one(k, _):
            to = (me + 2 * k) % SEQ
            remote(src.at[0, :, _rows((to // 2) * D, D)], dst, ss.at[s], sems.at[chip], at_seq(to))
            return 0

        lax.fori_loop(1, SEQ // 2, one, 0)

    send_key_heads(k_in, k_buf.at[mine], S_K, rs_k)
    send_heads(q_in, q_buf.at[mine], S_Q)
    send_key_heads(v_in, v_aug.at[mine, pl.ds(0, D)], S_V, rs_v)
    send_heads(g_in, g_aug.at[mine, pl.ds(0, D)], S_G)

    drain(seg_buf, rs.at[S_SEG])

    def documents(i, _):
        ids = seg_buf[pl.ds(i, 1), :].astype(F32)
        column = jnp.transpose(jnp.broadcast_to(ids, (D, D)))
        same = column == lane.astype(F32)
        rows = _rows(i * TOK, TOK)
        q_aug[rows, D:] = jnp.where(same, 1.0, 0.0).astype(BF16)
        k_aug[rows, D:] = jnp.where(same | (lane > 3), 0.0, FAR).astype(BF16)
        return 0

    lax.fori_loop(0, SEQ, documents, 0)

    def forward(k, sems, s, view):
        owner = (me - 2 * k + SEQ) % SEQ
        ref = view(_rows(owner * TOK, TOK))
        drain(ref, sems.at[owner // 2])
        remote(ref, ref, ss.at[s], rs.at[s], at_seq(sib))

    def forward_key(k, _):
        forward(k, rs_k, S_KF, lambda rows: k_buf.at[rows])
        return 0

    lax.fori_loop(0, SEQ // 2, forward_key, 0)
    half = pl.ds(0, LEN // 2)
    drain(k_buf.at[half], rs.at[S_KF])

    def norm_keys(i, _):
        rows = _rows(i * B, B)
        x = k_buf[rows, :].astype(F32)
        scaled = (x * _inverse_norm(x) * kg_in[...]).astype(BF16)
        k_aug[rows, :D] = scaled
        k_t[:, rows] = jnp.transpose(scaled)
        return 0

    lax.fori_loop(0, NB, norm_keys, 0)

    drain(q_buf, rs.at[S_Q])

    def norm_queries(i, _):
        rows = _rows(i * B, B)
        x = q_buf[rows, :].astype(F32)
        q_aug[rows, :D] = (x * _inverse_norm(x) * qg_in[...]).astype(BF16)
        return 0

    lax.fori_loop(0, NB, norm_queries, 0)

    causal = lax.broadcasted_iota(jnp.int32, (B, B), 0) <= lax.broadcasted_iota(jnp.int32, (B, B), 1)

    def scores(j, blocks):
        rows = _rows(j * B, B)
        k_block = k_aug[rows, :]
        for b in range(blocks):
            q_block = q_aug[_rows((j + b) * B, B), :]
            s = lax.dot_general(k_block, q_block, NT, preferred_element_type=F32)
            e = jnp.exp2(s * exponent_scale)
            if b == 0:
                e = jnp.where(causal, e, 0.0)
            e_buf[rows, b * B : (b + 1) * B] = e.astype(BF16)
        forward(j, rs_v, S_VF, lambda rows: v_aug.at[rows, pl.ds(0, D)])

    _grouped(scores)

    drain(v_aug.at[half, pl.ds(0, D)], rs.at[S_VF])

    def transpose_values(i, _):
        rows = _rows(i * B, B)
        v_t[:D, rows] = jnp.transpose(v_aug[rows, :D])
        return 0

    lax.fori_loop(0, NB, transpose_values, 0)

    def attend(j, blocks):
        rows = _rows(j * B, B)
        v_block = v_t[:, rows]
        for b in range(blocks):
            cols = _rows((j + b) * B, B)
            o_acc[:, cols] += _dot(v_block, e_buf[rows, b * B : (b + 1) * B])

    _grouped(attend)

    def return_tiles(t, i, src, out, s):
        cols = _rows(me * D, D)
        ours, other = 2 * i + core, 2 * i + 1 - core
        dst = out.at[0, :, cols]
        remote(src.at[_rows(other * TOK, TOK)], dst, ss.at[s], rs.at[s], at_seq(other))

        @pl.when(t == 0)
        def _():
            local(src.at[mine], dst, rs.at[s])

        @pl.when(t != 0)
        def _():
            remote(src.at[_rows(ours * TOK, TOK)], dst, ss.at[s], rs.at[s], at_seq(ours))

    def finish_attended(t, _):
        i = (chip + t) % NB
        cols = _rows(i * B, B)
        inverse = 1.0 / o_acc[D : D + 8, cols]
        inv_row[pl.ds(pl.multiple_of(i * 8, 8), 8), :] = inverse
        o = jnp.transpose((o_acc[:D, cols].reshape(D // 8, 8, B) * inverse[None]).reshape(D, B))
        o32[cols, :] = o
        o_bf[cols, :] = o.astype(BF16)
        return_tiles(t, i, o_bf, o_out, S_O)
        column = jnp.transpose(jnp.broadcast_to(inverse[None], (D // 8, 8, B)).reshape(D, B))
        inv_col[cols, :] = column
        q_inv[cols, :] = (q_aug[cols, :D].astype(F32) * (column * score_scale)).astype(BF16)
        return 0

    lax.fori_loop(0, NB, finish_attended, 0)

    drain(g_aug.at[pl.ds(0, LEN), pl.ds(0, D)], rs.at[S_G])
    lanes_b = lax.broadcasted_iota(jnp.int32, (B, D), 1)

    def row_terms(i, _):
        rows = _rows(i * B, B)
        g = g_aug[rows, :D].astype(F32)
        g_inv[rows, :] = (g * inv_col[rows, :]).astype(BF16)
        r = -jnp.sum(o32[rows, :] * g, axis=-1, keepdims=True)
        r1 = r.astype(BF16).astype(F32)
        r2 = (r - r1).astype(BF16).astype(F32)
        r3 = r - r1 - r2
        terms = jnp.where(lanes_b == 0, r1, jnp.where(lanes_b == 1, r2, jnp.where(lanes_b == 2, r3, 0.0)))
        g_aug[rows, D:] = terms.astype(BF16)
        return 0

    lax.fori_loop(0, NB, row_terms, 0)

    def backward(j, blocks):
        rows = _rows(j * B, B)
        v_block = v_aug[rows, :]
        k_block_t = k_t[:, rows]
        dk = dv = jnp.zeros((B, D), F32)
        for b in range(blocks):
            cols = _rows((j + b) * B, B)
            e = e_buf[rows, b * B : (b + 1) * B]
            gw = lax.dot_general(v_block, g_aug[cols, :], NT, preferred_element_type=F32)
            ds = (e.astype(F32) * gw).astype(BF16)
            dv = dv + _dot(e, g_inv[cols, :])
            dk = dk + _dot(ds, q_inv[cols, :])
            dq_acc[:, cols] += _dot(k_block_t, ds)
        dk_buf[rows, :] = dk
        dv_buf[rows, :] = dv

    def exchange(j):
        theirs = _rows((2 * j + 1 - core) * TOK, TOK)
        slot = _rows(j * TOK, TOK)
        remote(dk_buf.at[theirs], x_k.at[slot], ss.at[S_XK], rs_xk.at[j], at_seq(sib))
        remote(dv_buf.at[theirs], x_v.at[slot], ss.at[S_XV], rs_xv.at[j], at_seq(sib))

    def finish_keys(t):
        j = (chip + t) % NB
        owner = 2 * j + core
        ours, slot = _rows(owner * TOK, TOK), _rows(j * TOK, TOK)
        drain(x_k.at[slot], rs_xk.at[j])
        drain(x_v.at[slot], rs_xv.at[j])
        gv_bf[slot, :] = (dv_buf[ours, :] + x_v[slot, :]).astype(BF16)
        x = k_buf[ours, :].astype(F32)
        inverse = _inverse_norm(x)
        unit = x * inverse
        dk = dk_buf[ours, :] + x_k[slot, :]
        part[8:, :] += _fold(dk * unit)
        gk_bf[slot, :] = _norm_backward(dk, inverse, unit, kg_in[...]).astype(BF16)
        cols = _rows(chip * D, D)

        @pl.when(t == 0)
        def _():
            local(gk_bf.at[slot], dk_out.at[0, :, cols], rs.at[S_DK])
            local(gv_bf.at[slot], dv_out.at[0, :, cols], rs.at[S_DV])

        @pl.when(t != 0)
        def _():
            remote(gk_bf.at[slot], dk_out.at[0, :, cols], ss.at[S_DK], rs.at[S_DK], at_seq(owner))
            remote(gv_bf.at[slot], dv_out.at[0, :, cols], ss.at[S_DV], rs.at[S_DV], at_seq(owner))

    def backward_step(t, _):
        j = (chip + t) % NB
        for first, last, blocks in ((0, 4, BAND), (4, 6, 4), (6, 8, 2)):

            @pl.when((j >= first) & (j < last))
            def _(blocks=blocks):
                backward(j, blocks)

        exchange(j)

        @pl.when(t > 0)
        def _():
            finish_keys(t - 1)

        return 0

    lax.fori_loop(0, NB, backward_step, 0)

    def finish_queries(t, _):
        i = (chip + t) % NB
        rows = _rows(i * B, B)
        inverse_row = inv_row[pl.ds(pl.multiple_of(i * 8, 8), 8), :] * score_scale
        dq = jnp.transpose((dq_acc[:, rows].reshape(D // 8, 8, B) * inverse_row[None]).reshape(D, B))
        x = q_buf[rows, :].astype(F32)
        inverse = _inverse_norm(x)
        unit = x * inverse
        part[:8, :] += _fold(dq * unit)
        gq_bf[rows, :] = _norm_backward(dq, inverse, unit, qg_in[...]).astype(BF16)
        return_tiles(t, i, gq_bf, dq_out, S_DQ)
        return 0

    lax.fori_loop(0, NB, finish_queries, 0)
    finish_keys(NB - 1)

    totals = jnp.sum(part[...].reshape(2, 8, D), axis=1)
    gain_src[...] = jnp.concatenate([totals, jnp.zeros((6, D), F32)], axis=0)

    def send_gain(k, _):
        remote(gain_src, gain_seq.at[me], ss.at[S_GAIN], rs.at[S_GAIN], at_seq((me + k) % SEQ))
        return 0

    lax.fori_loop(1, SEQ, send_gain, 0)
    gain_seq[me] = gain_src[...]
    drain(gain_seq.at[pl.ds(0, SEQ - 1)], rs.at[S_GAIN])
    trajectory = jnp.sum(gain_seq[...], axis=0)
    z_src[...] = trajectory
    four = z // 4
    z_four[four] = trajectory
    remote(z_src, z_four.at[four], ss.at[S_Z4], rs.at[S_Z4], at_z(0, 4))
    remote(z_src, z_four.at[four], ss.at[S_Z4], rs.at[S_Z5], at_z(0, -4))
    ahead = z_four.at[(four + 1) % 4]
    drain(ahead, rs.at[S_Z5])
    remote(ahead, ahead, ss.at[S_Z4B], rs.at[S_Z4B], at_z(0, -4))
    drain(z_four.at[(four + 3) % 4], rs.at[S_Z4])
    drain(z_four.at[(four + 2) % 4], rs.at[S_Z4B])
    column_sum = z_four[0] + z_four[1] + z_four[2] + z_four[3]
    zq_src[...] = column_sum
    place = x_lo * 4 + z % 4
    z_all[place] = column_sum
    last_peers = [at_z(0, 1), at_z(0, -1), at_z(0, 2), at_z(1, 0), at_z(1, 1), at_z(1, -1), at_z(1, 2)]
    for peer in last_peers:
        remote(zq_src, z_all.at[place], ss.at[S_ZA], rs.at[S_ZA], peer)
    drain(z_all.at[pl.ds(0, 7)], rs.at[S_ZA])
    gain_out[...] = jnp.sum(z_all[...], axis=0)

    drain(o_out.at[0], rs.at[S_O])
    drain(dq_out.at[0], rs.at[S_DQ])
    drain(dk_out.at[0], rs.at[S_DK])
    drain(dv_out.at[0], rs.at[S_DV])
    most, some = pl.ds(0, LEN - TOK), pl.ds(0, LEN // 2 - TOK)
    drain(seg_buf.at[pl.ds(0, SEQ - 1)], ss.at[S_SEG])
    drain(k_buf.at[some], ss.at[S_K])
    drain(q_buf.at[most], ss.at[S_Q])
    drain(k_buf.at[some], ss.at[S_V])
    drain(q_buf.at[most], ss.at[S_G])
    drain(k_buf.at[half], ss.at[S_KF])
    drain(k_buf.at[half], ss.at[S_VF])
    drain(o_bf.at[most], ss.at[S_O])
    drain(gq_bf.at[most], ss.at[S_DQ])
    drain(x_k, ss.at[S_XK])
    drain(x_v, ss.at[S_XV])
    drain(gk_bf.at[some], ss.at[S_DK])
    drain(gv_bf.at[some], ss.at[S_DV])
    drain(gain_seq.at[pl.ds(0, SEQ - 1)], ss.at[S_GAIN])
    drain(z_four.at[pl.ds(0, 2)], ss.at[S_Z4])
    drain(z_four.at[0], ss.at[S_Z4B])
    drain(z_all.at[pl.ds(0, 7)], ss.at[S_ZA])


def shards(q_raw, key_unnormed, value_input, grad_attended, segment_ids, q_gain, key_norm_gain):
    hbm = pl.BlockSpec(memory_space=pl.ANY)
    vmem = pl.BlockSpec(memory_space=pltpu.VMEM)
    q_heads, kv_heads = q_raw.shape[2] // D, key_unnormed.shape[2] // D
    dma = pltpu.SemaphoreType.DMA
    out = pl.pallas_call(
        kernel,
        out_shape=[
            jax.ShapeDtypeStruct(q_raw.shape, BF16),
            jax.ShapeDtypeStruct(q_raw.shape, BF16),
            jax.ShapeDtypeStruct(key_unnormed.shape, BF16),
            jax.ShapeDtypeStruct(key_unnormed.shape, BF16),
            jax.ShapeDtypeStruct((8, D), F32),
        ],
        in_specs=[hbm] * 5 + [vmem] * 2,
        out_specs=[hbm] * 4 + [vmem],
        scratch_shapes=[
            pltpu.VMEM((LEN, D), BF16),
            pltpu.VMEM((LEN, D), BF16),
            pltpu.VMEM((LEN, 2 * D), BF16),
            pltpu.VMEM((PAD, 2 * D), BF16),
            pltpu.VMEM((SEQ, TOK), jnp.int32),
            pltpu.VMEM((PAD, 2 * D), BF16),
            pltpu.VMEM((LEN, 2 * D), BF16),
            pltpu.VMEM((D, LEN), BF16),
            pltpu.VMEM((D + ONES, LEN), BF16),
            pltpu.VMEM((LEN, BAND * B), BF16),
            pltpu.VMEM((D + ONES, PAD), F32),
            pltpu.VMEM((LEN, D), F32),
            pltpu.VMEM((LEN, D), BF16),
            pltpu.VMEM((LEN, D), F32),
            pltpu.VMEM((NB * 8, B), F32),
            pltpu.VMEM((PAD, D), BF16),
            pltpu.VMEM((PAD, D), BF16),
            pltpu.VMEM((D, PAD), F32),
            pltpu.VMEM((LEN, D), F32),
            pltpu.VMEM((LEN, D), F32),
            pltpu.VMEM((LEN // 2, D), F32),
            pltpu.VMEM((LEN // 2, D), F32),
            pltpu.VMEM((LEN, D), BF16),
            pltpu.VMEM((LEN // 2, D), BF16),
            pltpu.VMEM((LEN // 2, D), BF16),
            pltpu.VMEM((16, D), F32),
            pltpu.VMEM((8, D), F32),
            pltpu.VMEM((SEQ, 8, D), F32),
            pltpu.VMEM((8, D), F32),
            pltpu.VMEM((4, 8, D), F32),
            pltpu.VMEM((8, D), F32),
            pltpu.VMEM((8, 8, D), F32),
            dma((18,)),
            dma((18,)),
            dma((8,)),
            dma((8,)),
            dma((8,)),
            dma((8,)),
        ],
        compiler_params=pltpu.CompilerParams(
            collective_id=0, has_side_effects=True, vmem_limit_bytes=52 << 20
        ),
        name="attention",
    )(
        q_raw,
        key_unnormed,
        value_input,
        grad_attended,
        segment_ids,
        q_gain.reshape(1, D),
        key_norm_gain.reshape(1, D),
    )
    attended, grad_q, grad_k, grad_value, gains = out
    tokens = lax.axis_size("dp") * lax.axis_size("seq") * q_raw.shape[1]
    grad_q_gain = gains[0] / math.sqrt(tokens * q_heads)
    key_gain_gradient = gains[1] / math.sqrt(tokens * kv_heads)
    return attended, grad_q, grad_k, grad_value, grad_q_gain, key_gain_gradient


def solution(mesh):
    tokens = P("dp", "seq", None)
    in_specs = (tokens, tokens, tokens, tokens, P("dp", "seq"), P(), P())
    out_specs = (tokens, tokens, tokens, tokens, P(), P())
    return jax.shard_map(shards, mesh=mesh, in_specs=in_specs, out_specs=out_specs, check_vma=False)
```

```python
import functools
import math

import jax
import jax.numpy as jnp
from jax import lax
from jax.experimental import pallas as pl
from jax.experimental.pallas import tpu as pltpu
from jax.sharding import PartitionSpec as P

MESH = pl.DeviceIdType.MESH
EPSILON = 1e-06
D = 128
TOK = 128
SEQ = 16
HEADS_KV = 8
LEN = TOK * SEQ
B = 256
NB = LEN // B
STEPS = 2
BAND = 5
ONES = 16
FAR = -16384.0
F32, BF16 = jnp.float32, jnp.bfloat16
NT = (((1,), (1,)), ((), ()))


def _rows(start, count):
    return pl.ds(pl.multiple_of(start, count), count)


def _dot(a, b):
    return jnp.dot(a, b, preferred_element_type=F32)


def _inverse_norm(x):
    return lax.rsqrt(jnp.mean(x * x, axis=-1, keepdims=True) + EPSILON)


def _norm_backward(grad, inverse, unit, gain):
    scaled = grad * gain
    return inverse * (scaled - unit * jnp.mean(scaled * unit, axis=-1, keepdims=True))


def _fold(x):
    return jnp.sum(x.reshape(x.shape[0] // 8, 8, D), axis=0)


def _blocks(j):
    return range(j, min(j + BAND, NB))


def _first_key(i):
    return max(0, i - BAND + 1)


def kernel(
    q_in, k_in, v_in, g_in, seg_in, qg_in, kg_in,
    o_out, dq_out, dk_out, dv_out, gain_out,
    q_buf, k_buf, v_aug, g_aug, seg_buf, q_aug, k_aug, k_t, v_t, e_keys, e_queries, ds_keys, q_unit, q_norm,
    o32, o_bf, inv_col, inv_row, g_inv, q_inv, dq_acc, dk_buf, dv_buf, x_k, x_v,
    gq_bf, gk_bf, gv_bf, qg, kg, part, gain_seq, z_src, z_four, zq_src, z_all,
    ss, rs, rs_k, rs_v, rs_xk, rs_xv,
):
    dp, me = lax.axis_index("dp"), lax.axis_index("seq")
    chip, core = me // 2, me % 2
    sib = me + 1 - 2 * core
    x_lo, z = dp // 16, dp % 16
    score_scale = D ** (-0.5)
    exponent_scale = score_scale * math.log2(math.e)

    (S_SEG, S_K, S_Q, S_V, S_G, S_KF, S_VF, S_O, S_DQ, S_XK, S_XV, S_DK, S_DV, S_GAIN, S_Z4, S_Z4B, S_ZA, S_Z5, S_QG, S_KG) = range(20)

    def at_seq(i):
        return (dp, i)

    def at_z(dx, dz):
        return (((x_lo + dx) % 2) * 16 + (z + dz + 16) % 16, me)

    z_peers = [at_z(0, 4), at_z(0, -4), at_z(0, 1), at_z(0, -1), at_z(0, 2), at_z(0, -2)]
    z_peers += [at_z(1, 0), at_z(1, 1), at_z(1, -1), at_z(1, 2), at_z(1, -2)]

    barrier = pltpu.get_barrier_semaphore()

    def greet(k, _):
        pl.semaphore_signal(barrier, inc=1, device_id=at_seq((me + k) % SEQ), device_id_type=MESH)
        return 0

    lax.fori_loop(1, SEQ, greet, 0)
    for peer in z_peers:
        pl.semaphore_signal(barrier, inc=1, device_id=peer, device_id_type=MESH)

    lane = lax.broadcasted_iota(jnp.int32, (D, D), 1)
    v_aug[:, D:] = jnp.ones((LEN, D), BF16)
    v_t[D:, :] = jnp.ones((ONES, LEN), BF16)
    pltpu.make_async_copy(qg_in, qg, rs.at[S_QG]).start()
    pltpu.make_async_copy(kg_in, kg, rs.at[S_KG]).start()

    pl.semaphore_wait(barrier, SEQ - 1 + len(z_peers))

    def remote(src, dst, send, recv, peer):
        pltpu.make_async_remote_copy(src_ref=src, dst_ref=dst, send_sem=send, recv_sem=recv, device_id=peer, device_id_type=MESH).start()

    def local(src, dst, sem):
        pltpu.make_async_copy(src, dst, sem).start()

    def drain(ref, sem):
        pltpu.make_async_copy(ref, ref, sem).wait()

    mine = _rows(me * TOK, TOK)

    def send_seg(k, _):
        remote(seg_in, seg_buf.at[pl.ds(me, 1)], ss.at[S_SEG], rs.at[S_SEG], at_seq((me + k) % SEQ))
        return 0

    local(seg_in, seg_buf.at[pl.ds(me, 1)], rs.at[S_SEG])
    lax.fori_loop(1, SEQ, send_seg, 0)

    def send_heads(src, dst, s):
        local(src.at[0, :, _rows(me * D, D)], dst, rs.at[s])

        def one(k, _):
            to = (me + k) % SEQ
            remote(src.at[0, :, _rows(to * D, D)], dst, ss.at[s], rs.at[s], at_seq(to))
            return 0

        lax.fori_loop(1, SEQ, one, 0)

    def send_key_heads(src, dst, s, sems):
        local(src.at[0, :, _rows(chip * D, D)], dst, sems.at[chip])

        def one(k, _):
            to = (me + 2 * k) % SEQ
            remote(src.at[0, :, _rows((to // 2) * D, D)], dst, ss.at[s], sems.at[chip], at_seq(to))
            return 0

        lax.fori_loop(1, SEQ // 2, one, 0)

    send_key_heads(k_in, k_buf.at[mine], S_K, rs_k)
    send_key_heads(v_in, v_aug.at[mine, pl.ds(0, D)], S_V, rs_v)
    send_heads(q_in, q_buf.at[mine], S_Q)
    send_heads(g_in, g_aug.at[mine, pl.ds(0, D)], S_G)

    drain(qg, rs.at[S_QG])
    drain(kg, rs.at[S_KG])
    drain(seg_buf, rs.at[S_SEG])

    def documents(i, _):
        ids = seg_buf[pl.ds(i, 1), :].astype(F32)
        column = jnp.transpose(jnp.broadcast_to(ids, (D, D)))
        same = column == lane.astype(F32)
        rows = _rows(i * TOK, TOK)
        q_aug[rows, D:] = jnp.where(same, 1.0, 0.0).astype(BF16)
        k_aug[rows, D:] = jnp.where(same | (lane > 3), 0.0, FAR).astype(BF16)
        return 0

    lax.fori_loop(0, SEQ, documents, 0, unroll=4)

    def forward(k, sems, s, view):
        owner = (me - 2 * k + SEQ) % SEQ
        ref = view(_rows(owner * TOK, TOK))
        drain(ref, sems.at[owner // 2])
        remote(ref, ref, ss.at[s], rs.at[s], at_seq(sib))

    def forward_key(k, _):
        forward(k, rs_k, S_KF, lambda rows: k_buf.at[rows])
        return 0

    lax.fori_loop(0, SEQ // 2, forward_key, 0)
    half = pl.ds(0, LEN // 2)
    drain(k_buf.at[half], rs.at[S_KF])

    def norm_keys(i, _):
        rows = _rows(i * B, B)
        x = k_buf[rows, :].astype(F32)
        scaled = (x * _inverse_norm(x) * kg[...]).astype(BF16)
        k_aug[rows, :D] = scaled
        k_t[:, rows] = jnp.transpose(scaled)
        return 0

    lax.fori_loop(0, NB, norm_keys, 0, unroll=4)

    def forward_value(k, _):
        forward(k, rs_v, S_VF, lambda rows: v_aug.at[rows, pl.ds(0, D)])
        return 0

    lax.fori_loop(0, SEQ // 2, forward_value, 0)
    drain(v_aug.at[half, pl.ds(0, D)], rs.at[S_VF])

    def transpose_values(i, _):
        rows = _rows(i * B, B)
        v_t[:D, rows] = jnp.transpose(v_aug[rows, :D])
        return 0

    lax.fori_loop(0, NB, transpose_values, 0, unroll=4)

    drain(q_buf, rs.at[S_Q])

    def norm_queries(i, _):
        rows = _rows(i * B, B)
        x = q_buf[rows, :].astype(F32)
        inverse = _inverse_norm(x)
        unit = x * inverse
        q_norm[rows, :] = jnp.broadcast_to(inverse, (B, D))
        q_unit[rows, :] = unit
        q_aug[rows, :D] = (unit * qg[...]).astype(BF16)
        return 0

    lax.fori_loop(0, NB, norm_queries, 0, unroll=4)
    causal = lax.broadcasted_iota(jnp.int32, (B, B), 0) <= lax.broadcasted_iota(jnp.int32, (B, B), 1)

    for j in range(NB):
        k_block = k_aug[j * B : (j + 1) * B, :]
        for i in _blocks(j):
            s = lax.dot_general(k_block, q_aug[i * B : (i + 1) * B, :], NT, preferred_element_type=F32)
            e = jnp.exp2(s * exponent_scale)
            if i == j:
                e = jnp.where(causal, e, 0.0)
            e = e.astype(BF16)
            e_keys[j * B : (j + 1) * B, (i - j) * B : (i - j + 1) * B] = e
            at = (i * BAND + j - _first_key(i)) * B
            e_queries[at : at + B, :] = e

    for i in range(NB):
        first, rows = _first_key(i), slice(i * B, (i + 1) * B)
        keys = (i + 1 - first) * B
        o_t = _dot(v_t[:, first * B : (i + 1) * B], e_queries[i * BAND * B : i * BAND * B + keys, :])
        inverse = 1.0 / o_t[D : D + 8, :]
        inv_row[i * 8 : (i + 1) * 8, :] = inverse
        o = jnp.transpose((o_t[:D, :].reshape(D // 8, 8, B) * inverse[None]).reshape(D, B))
        o32[rows, :] = o
        o_bf[rows, :] = o.astype(BF16)
        column = jnp.transpose(jnp.broadcast_to(inverse[None], (D // 8, 8, B)).reshape(D, B))
        inv_col[rows, :] = column
        q_inv[rows, :] = (q_aug[rows, :D].astype(F32) * (column * score_scale)).astype(BF16)

    def return_tiles(src, out, s):
        dst = out.at[0, :, _rows(me * D, D)]
        local(src.at[mine], dst, rs.at[s])
        remote(src.at[_rows(sib * TOK, TOK)], dst, ss.at[s], rs.at[s], at_seq(sib))

        def one(t, _):
            i = (chip + t) % NB
            ours, other = 2 * i + core, 2 * i + 1 - core
            remote(src.at[_rows(ours * TOK, TOK)], dst, ss.at[s], rs.at[s], at_seq(ours))
            remote(src.at[_rows(other * TOK, TOK)], dst, ss.at[s], rs.at[s], at_seq(other))
            return 0

        lax.fori_loop(1, NB, one, 0)

    return_tiles(o_bf, o_out, S_O)

    drain(g_aug.at[:, pl.ds(0, D)], rs.at[S_G])
    lanes_b = lax.broadcasted_iota(jnp.int32, (B, D), 1)

    for i in range(NB):
        rows = slice(i * B, (i + 1) * B)
        g = g_aug[rows, :D].astype(F32)
        g_inv[rows, :] = (g * inv_col[rows, :]).astype(BF16)
        r = -jnp.sum(o32[rows, :] * g, axis=-1, keepdims=True)
        r1 = r.astype(BF16).astype(F32)
        r2 = (r - r1).astype(BF16).astype(F32)
        r3 = r - r1 - r2
        terms = jnp.where(lanes_b == 0, r1, jnp.where(lanes_b == 1, r2, jnp.where(lanes_b == 2, r3, 0.0)))
        g_aug[rows, D:] = terms.astype(BF16)

    gain_part = jnp.zeros((8, D), F32)
    for j in range(NB):
        rows, queries = slice(j * B, (j + 1) * B), slice(j * B, (_blocks(j)[-1] + 1) * B)
        span = len(_blocks(j)) * B
        v_block = v_aug[rows, :]
        for i in _blocks(j):
            cols = slice((i - j) * B, (i - j + 1) * B)
            gw = lax.dot_general(v_block, g_aug[i * B : (i + 1) * B, :], NT, preferred_element_type=F32)
            ds_keys[j % 2, :, cols] = (e_keys[rows, cols].astype(F32) * gw).astype(BF16)
        ds = ds_keys[j % 2, :, :span]
        dv_buf[rows, :] = _dot(e_keys[rows, :span], g_inv[queries, :])
        dk = _dot(ds, q_inv[queries, :])
        dk_buf[rows, :] = dk
        gain_part = gain_part + _fold(dk * k_aug[rows, :D].astype(F32))
        part_dq = _dot(k_t[:, rows], ds)
        if j == 0:
            dq_acc[:, queries] = part_dq
        else:
            old = slice(queries.start, min(queries.stop, (j + BAND - 1) * B))
            width = old.stop - old.start
            dq_acc[:, old] += part_dq[:, :width]
            if width < span:
                dq_acc[:, old.stop : queries.stop] = part_dq[:, width:]
        theirs = _rows((2 * j + 1 - core) * TOK, TOK)
        slot = pl.ds(j * TOK, TOK)
        remote(dk_buf.at[theirs], x_k.at[slot], ss.at[S_XK], rs_xk.at[j], at_seq(sib))
        remote(dv_buf.at[theirs], x_v.at[slot], ss.at[S_XV], rs_xv.at[j], at_seq(sib))
    part[...] = gain_part

    def send_gain(k, _):
        remote(part, gain_seq.at[me], ss.at[S_GAIN], rs.at[S_GAIN], at_seq((me + k) % SEQ))
        return 0

    lax.fori_loop(1, SEQ, send_gain, 0)
    gain_seq[me] = part[...]

    for i in range(NB):
        rows = slice(i * B, (i + 1) * B)
        inverse_row = inv_row[i * 8 : (i + 1) * 8, :] * score_scale
        dq = jnp.transpose((dq_acc[:, rows].reshape(D // 8, 8, B) * inverse_row[None]).reshape(D, B))
        gq_bf[rows, :] = _norm_backward(dq, q_norm[rows, :], q_unit[rows, :], qg[...]).astype(BF16)
    return_tiles(gq_bf, dq_out, S_DQ)

    for j in range(NB):
        ours, slot = _rows((2 * j + core) * TOK, TOK), pl.ds(j * TOK, TOK)
        drain(x_k.at[slot], rs_xk.at[j])
        drain(x_v.at[slot], rs_xv.at[j])
        gv_bf[slot, :] = (dv_buf[ours, :] + x_v[slot, :]).astype(BF16)
        x = k_buf[ours, :].astype(F32)
        inverse = _inverse_norm(x)
        gk_bf[slot, :] = _norm_backward(dk_buf[ours, :] + x_k[slot, :], inverse, x * inverse, kg[...]).astype(BF16)

    key_cols = _rows(chip * D, D)
    dk_dst, dv_dst = dk_out.at[0, :, key_cols], dv_out.at[0, :, key_cols]
    local(gk_bf.at[_rows(chip * TOK, TOK)], dk_dst, rs.at[S_DK])
    local(gv_bf.at[_rows(chip * TOK, TOK)], dv_dst, rs.at[S_DV])

    def return_keys(t, _):
        j = (chip + t) % NB
        slot = _rows(j * TOK, TOK)
        remote(gk_bf.at[slot], dk_dst, ss.at[S_DK], rs.at[S_DK], at_seq(2 * j + core))
        remote(gv_bf.at[slot], dv_dst, ss.at[S_DV], rs.at[S_DV], at_seq(2 * j + core))
        return 0

    lax.fori_loop(1, NB, return_keys, 0)

    drain(gain_seq.at[pl.ds(0, SEQ - 1)], rs.at[S_GAIN])
    trajectory = jnp.sum(gain_seq[...], axis=0)
    z_src[...] = trajectory
    four = z // 4
    z_four[four] = trajectory
    remote(z_src, z_four.at[four], ss.at[S_Z4], rs.at[S_Z4], at_z(0, 4))
    remote(z_src, z_four.at[four], ss.at[S_Z4], rs.at[S_Z5], at_z(0, -4))
    ahead = z_four.at[(four + 1) % 4]
    drain(ahead, rs.at[S_Z5])
    remote(ahead, ahead, ss.at[S_Z4B], rs.at[S_Z4B], at_z(0, -4))
    drain(z_four.at[(four + 3) % 4], rs.at[S_Z4])
    drain(z_four.at[(four + 2) % 4], rs.at[S_Z4B])
    column_sum = z_four[0] + z_four[1] + z_four[2] + z_four[3]
    zq_src[...] = column_sum
    place = x_lo * 4 + z % 4
    z_all[place] = column_sum
    last_peers = [at_z(0, 1), at_z(0, -1), at_z(0, 2), at_z(1, 0), at_z(1, 1), at_z(1, -1), at_z(1, 2)]
    for peer in last_peers:
        remote(zq_src, z_all.at[place], ss.at[S_ZA], rs.at[S_ZA], peer)
    drain(z_all.at[pl.ds(0, 7)], rs.at[S_ZA])
    total = jnp.sum(jnp.sum(z_all[...], axis=0), axis=0, keepdims=True)
    gain_out[0:1, :] = total / qg[...]
    gain_out[1:2, :] = total / kg[...]

    drain(o_out.at[0], rs.at[S_O])
    drain(dq_out.at[0], rs.at[S_DQ])
    drain(dk_out.at[0], rs.at[S_DK])
    drain(dv_out.at[0], rs.at[S_DV])
    most, some = pl.ds(0, LEN - TOK), pl.ds(0, LEN // 2 - TOK)
    drain(seg_buf.at[pl.ds(0, SEQ - 1)], ss.at[S_SEG])
    drain(k_buf.at[some], ss.at[S_K])
    drain(q_buf.at[most], ss.at[S_Q])
    drain(k_buf.at[some], ss.at[S_V])
    drain(q_buf.at[most], ss.at[S_G])
    drain(k_buf.at[half], ss.at[S_KF])
    drain(k_buf.at[half], ss.at[S_VF])
    drain(o_bf.at[most], ss.at[S_O])
    drain(gq_bf.at[most], ss.at[S_DQ])
    drain(x_k, ss.at[S_XK])
    drain(x_v, ss.at[S_XV])
    drain(gk_bf.at[some], ss.at[S_DK])
    drain(gv_bf.at[some], ss.at[S_DV])
    drain(gain_seq.at[pl.ds(0, SEQ - 1)], ss.at[S_GAIN])
    drain(z_four.at[pl.ds(0, 2)], ss.at[S_Z4])
    drain(z_four.at[0], ss.at[S_Z4B])
    drain(z_all.at[pl.ds(0, 7)], ss.at[S_ZA])


def finish(o_in, dq_in, dk_in, dv_in, gains, o_out, dq_out, dk_out, dv_out, q_out, k_out, *, q_scale, k_scale):
    for src, dst in ((o_in, o_out), (dq_in, dq_out), (dk_in, dk_out), (dv_in, dv_out)):
        dst[...] = src[...]
    q_out[...] = gains[0:1, :] * q_scale
    k_out[...] = gains[1:2, :] * k_scale


def shards(q_raw, key_unnormed, value_input, grad_attended, segment_ids, q_gain, key_norm_gain):
    hbm = pl.BlockSpec(memory_space=pltpu.HBM)
    anywhere = pl.BlockSpec(memory_space=pl.ANY)
    vmem = pl.BlockSpec(memory_space=pltpu.VMEM)
    q_heads, kv_heads = q_raw.shape[2] // D, key_unnormed.shape[2] // D
    dma = pltpu.SemaphoreType.DMA
    results = [
        jax.ShapeDtypeStruct(q_raw.shape, BF16),
        jax.ShapeDtypeStruct(q_raw.shape, BF16),
        jax.ShapeDtypeStruct(key_unnormed.shape, BF16),
        jax.ShapeDtypeStruct(key_unnormed.shape, BF16),
    ]
    staged = pl.pallas_call(
        kernel,
        out_shape=results + [jax.ShapeDtypeStruct((8, D), F32)],
        in_specs=[hbm] * 7,
        out_specs=[anywhere] * 4 + [vmem],
        scratch_shapes=[
            pltpu.VMEM((LEN, D), BF16),
            pltpu.VMEM((LEN, D), BF16),
            pltpu.VMEM((LEN, 2 * D), BF16),
            pltpu.VMEM((LEN, 2 * D), BF16),
            pltpu.VMEM((SEQ, TOK), jnp.int32),
            pltpu.VMEM((LEN, 2 * D), BF16),
            pltpu.VMEM((LEN, 2 * D), BF16),
            pltpu.VMEM((D, LEN), BF16),
            pltpu.VMEM((D + ONES, LEN), BF16),
            pltpu.VMEM((LEN, BAND * B), BF16),
            pltpu.VMEM((NB * BAND * B, B), BF16),
            pltpu.VMEM((2, B, BAND * B), BF16),
            pltpu.VMEM((LEN, D), F32),
            pltpu.VMEM((LEN, D), F32),
            pltpu.VMEM((LEN, D), F32),
            pltpu.VMEM((LEN, D), BF16),
            pltpu.VMEM((LEN, D), F32),
            pltpu.VMEM((NB * 8, B), F32),
            pltpu.VMEM((LEN, D), BF16),
            pltpu.VMEM((LEN, D), BF16),
            pltpu.VMEM((D, LEN), F32),
            pltpu.VMEM((LEN, D), F32),
            pltpu.VMEM((LEN, D), F32),
            pltpu.VMEM((LEN // 2, D), F32),
            pltpu.VMEM((LEN // 2, D), F32),
            pltpu.VMEM((LEN, D), BF16),
            pltpu.VMEM((LEN // 2, D), BF16),
            pltpu.VMEM((LEN // 2, D), BF16),
            pltpu.VMEM((1, D), F32),
            pltpu.VMEM((1, D), F32),
            pltpu.VMEM((8, D), F32),
            pltpu.VMEM((SEQ, 8, D), F32),
            pltpu.VMEM((8, D), F32),
            pltpu.VMEM((4, 8, D), F32),
            pltpu.VMEM((8, D), F32),
            pltpu.VMEM((8, 8, D), F32),
            dma((20,)),
            dma((20,)),
            dma((8,)),
            dma((8,)),
            dma((8,)),
            dma((8,)),
        ],
        compiler_params=pltpu.CompilerParams(
            collective_id=0, has_side_effects=True, vmem_limit_bytes=60 << 20
        ),
        name="attention",
    )(
        q_raw,
        key_unnormed,
        value_input,
        grad_attended,
        segment_ids,
        q_gain.reshape(1, D),
        key_norm_gain.reshape(1, D),
    )
    tokens = lax.axis_size("dp") * lax.axis_size("seq") * q_raw.shape[1]
    row = jax.ShapeDtypeStruct((1, D), F32)
    tiles = [pl.BlockSpec((1, TOK // STEPS, r.shape[2]), lambda t: (0, t, 0)) for r in results]
    rows = [pl.BlockSpec((count, D), lambda t: (0, 0)) for count in (8, 1, 1)]
    *tiles, grad_q_gain, key_gain_gradient = pl.pallas_call(
        functools.partial(finish, q_scale=(tokens * q_heads) ** -0.5, k_scale=(tokens * kv_heads) ** -0.5),
        out_shape=results + [row, row],
        grid=(STEPS,),
        in_specs=tiles + rows[:1],
        out_specs=tiles + rows[1:],
        name="finish",
    )(*staged)
    return *tiles, grad_q_gain.reshape(D), key_gain_gradient.reshape(D)


def solution(mesh):
    tokens = P("dp", "seq", None)
    in_specs = (tokens, tokens, tokens, tokens, P("dp", "seq"), P(), P())
    out_specs = (tokens, tokens, tokens, tokens, P(), P())
    return jax.shard_map(shards, mesh=mesh, in_specs=in_specs, out_specs=out_specs, check_vma=False)
```

```python
import functools
import math

import jax
import jax.numpy as jnp
from jax import lax
from jax.experimental import pallas as pl
from jax.experimental.pallas import tpu as pltpu
from jax.sharding import PartitionSpec as P

MESH = pl.DeviceIdType.MESH
EPSILON = 1e-06
D = 128
TOK = 128
SEQ = 16
DP = 32
HEADS_KV = 8
LEN = TOK * SEQ
B = 256
NB = LEN // B
STEPS = 2
BAND = 5
ONES = 16
FAR = -16384.0
F32, BF16 = jnp.float32, jnp.bfloat16
NT = (((1,), (1,)), ((), ()))


def _rows(start, count):
    return pl.ds(pl.multiple_of(start, count), count)


def _dot(a, b):
    return jnp.dot(a, b, preferred_element_type=F32)


def _inverse_norm(x):
    return lax.rsqrt(jnp.mean(x * x, axis=-1, keepdims=True) + EPSILON)


def _norm_backward(grad, inverse, unit, gain):
    scaled = grad * gain
    return inverse * (scaled - unit * jnp.mean(scaled * unit, axis=-1, keepdims=True))


def _fold(x):
    return jnp.sum(x.reshape(x.shape[0] // 8, 8, D), axis=0)


def _blocks(j):
    return range(j, min(j + BAND, NB))


def _first_key(i):
    return max(0, i - BAND + 1)


def kernel(
    q_in, k_in, v_in, g_in, seg_in, qg_in, kg_in,
    o_out, dq_out, dk_out, dv_out, gain_out,
    q_buf, k_buf, v_aug, g_aug, seg_buf, q_aug, k_aug, k_t, v_t, e_keys, e_queries, ds_keys, q_unit, q_norm,
    o32, o_bf, inv_col, inv_row, g_inv, q_inv, dq_acc, dk_buf, dv_buf, x_k, x_v,
    gq_bf, gk_bf, gv_bf, qg, kg, part, pair, gain_dp, gain_sum, gain_seq,
    ss, rs, rs_k, rs_v, rs_xk, rs_xv, opened,
):
    dp, me = lax.axis_index("dp"), lax.axis_index("seq")
    chip, core = me // 2, me % 2
    sib = me + 1 - 2 * core
    score_scale = D ** (-0.5)
    exponent_scale = score_scale * math.log2(math.e)

    (S_SEG, S_K, S_Q, S_V, S_G, S_KF, S_VF, S_O, S_DQ, S_XK, S_XV, S_DK, S_DV, S_PAIR, S_DP, S_GAIN, S_QG, S_KG) = range(18)

    def at_seq(i):
        return (dp, i)

    def at_dp(k):
        return ((dp + k) % DP, me)

    barrier = pltpu.get_barrier_semaphore()

    def greet(k, _):
        to = 2 * ((chip + k) % NB) + 1

        @pl.when(to != me)
        def _():
            pl.semaphore_signal(barrier, inc=1, device_id=at_seq(to), device_id_type=MESH)

        return 0

    lax.fori_loop(0, NB, greet, 0)

    lane = lax.broadcasted_iota(jnp.int32, (D, D), 1)
    v_aug[:, D:] = jnp.ones((LEN, D), BF16)
    v_t[D:, :] = jnp.ones((ONES, LEN), BF16)
    pltpu.make_async_copy(qg_in, qg, rs.at[S_QG]).start()
    pltpu.make_async_copy(kg_in, kg, rs.at[S_KG]).start()

    @pl.when(core == 1)
    def _():
        pl.semaphore_wait(barrier, SEQ - 1)
        pl.semaphore_signal(opened, inc=1, device_id=at_seq(sib), device_id_type=MESH)

    @pl.when(core == 0)
    def _():
        pl.semaphore_wait(opened, 1)


    def remote(src, dst, send, recv, peer):
        pltpu.make_async_remote_copy(src_ref=src, dst_ref=dst, send_sem=send, recv_sem=recv, device_id=peer, device_id_type=MESH).start()

    def local(src, dst, sem):
        pltpu.make_async_copy(src, dst, sem).start()

    def drain(ref, sem):
        pltpu.make_async_copy(ref, ref, sem).wait()

    mine = _rows(me * TOK, TOK)

    def send_seg(k, _):
        remote(seg_in, seg_buf.at[pl.ds(me, 1)], ss.at[S_SEG], rs.at[S_SEG], at_seq((me + k) % SEQ))
        return 0

    local(seg_in, seg_buf.at[pl.ds(me, 1)], rs.at[S_SEG])
    lax.fori_loop(1, SEQ, send_seg, 0)

    def send_heads(src, dst, s):
        local(src.at[0, :, _rows(me * D, D)], dst, rs.at[s])

        def one(k, _):
            to = (me + k) % SEQ
            remote(src.at[0, :, _rows(to * D, D)], dst, ss.at[s], rs.at[s], at_seq(to))
            return 0

        lax.fori_loop(1, SEQ, one, 0)

    def send_key_heads(src, dst, s, sems):
        local(src.at[0, :, _rows(chip * D, D)], dst, sems.at[chip])

        def one(k, _):
            to = (me + 2 * k) % SEQ
            remote(src.at[0, :, _rows((to // 2) * D, D)], dst, ss.at[s], sems.at[chip], at_seq(to))
            return 0

        lax.fori_loop(1, SEQ // 2, one, 0)

    send_key_heads(k_in, k_buf.at[mine], S_K, rs_k)
    send_key_heads(v_in, v_aug.at[mine, pl.ds(0, D)], S_V, rs_v)
    send_heads(q_in, q_buf.at[mine], S_Q)
    send_heads(g_in, g_aug.at[mine, pl.ds(0, D)], S_G)

    @pl.when(core == 0)
    def _():
        def greet_dp(k, _):
            pl.semaphore_signal(barrier, inc=1, device_id=at_dp(k), device_id_type=MESH)
            return 0

        lax.fori_loop(1, DP, greet_dp, 0)

    drain(qg, rs.at[S_QG])
    drain(kg, rs.at[S_KG])
    drain(seg_buf, rs.at[S_SEG])

    def documents(i, _):
        ids = seg_buf[pl.ds(i, 1), :].astype(F32)
        column = jnp.transpose(jnp.broadcast_to(ids, (D, D)))
        same = column == lane.astype(F32)
        rows = _rows(i * TOK, TOK)
        q_aug[rows, D:] = jnp.where(same, 1.0, 0.0).astype(BF16)
        k_aug[rows, D:] = jnp.where(same | (lane > 3), 0.0, FAR).astype(BF16)
        return 0

    lax.fori_loop(0, SEQ, documents, 0, unroll=4)

    def forward(k, sems, s, view):
        owner = (me - 2 * k + SEQ) % SEQ
        ref = view(_rows(owner * TOK, TOK))
        drain(ref, sems.at[owner // 2])
        remote(ref, ref, ss.at[s], rs.at[s], at_seq(sib))

    def forward_key(k, _):
        forward(k, rs_k, S_KF, lambda rows: k_buf.at[rows])
        return 0

    lax.fori_loop(0, SEQ // 2, forward_key, 0)
    half = pl.ds(0, LEN // 2)
    drain(k_buf.at[half], rs.at[S_KF])

    def norm_keys(i, _):
        rows = _rows(i * B, B)
        x = k_buf[rows, :].astype(F32)
        scaled = (x * _inverse_norm(x) * kg[...]).astype(BF16)
        k_aug[rows, :D] = scaled
        k_t[:, rows] = jnp.transpose(scaled)
        return 0

    lax.fori_loop(0, NB, norm_keys, 0, unroll=4)

    def forward_value(k, _):
        forward(k, rs_v, S_VF, lambda rows: v_aug.at[rows, pl.ds(0, D)])
        return 0

    lax.fori_loop(0, SEQ // 2, forward_value, 0)
    drain(v_aug.at[half, pl.ds(0, D)], rs.at[S_VF])

    def transpose_values(i, _):
        rows = _rows(i * B, B)
        v_t[:D, rows] = jnp.transpose(v_aug[rows, :D])
        return 0

    lax.fori_loop(0, NB, transpose_values, 0, unroll=4)

    drain(q_buf, rs.at[S_Q])

    def norm_queries(i, _):
        rows = _rows(i * B, B)
        x = q_buf[rows, :].astype(F32)
        inverse = _inverse_norm(x)
        unit = x * inverse
        q_norm[rows, :] = jnp.broadcast_to(inverse, (B, D))
        q_unit[rows, :] = unit
        q_aug[rows, :D] = (unit * qg[...]).astype(BF16)
        return 0

    lax.fori_loop(0, NB, norm_queries, 0, unroll=4)
    causal = lax.broadcasted_iota(jnp.int32, (B, B), 0) <= lax.broadcasted_iota(jnp.int32, (B, B), 1)

    for j in range(NB):
        k_block = k_aug[j * B : (j + 1) * B, :]
        for i in _blocks(j):
            s = lax.dot_general(k_block, q_aug[i * B : (i + 1) * B, :], NT, preferred_element_type=F32)
            e = jnp.exp2(s * exponent_scale)
            if i == j:
                e = jnp.where(causal, e, 0.0)
            e = e.astype(BF16)
            e_keys[j * B : (j + 1) * B, (i - j) * B : (i - j + 1) * B] = e
            at = (i * BAND + j - _first_key(i)) * B
            e_queries[at : at + B, :] = e

    for i in range(NB):
        first, rows = _first_key(i), slice(i * B, (i + 1) * B)
        keys = (i + 1 - first) * B
        o_t = _dot(v_t[:, first * B : (i + 1) * B], e_queries[i * BAND * B : i * BAND * B + keys, :])
        inverse = 1.0 / o_t[D : D + 8, :]
        inv_row[i * 8 : (i + 1) * 8, :] = inverse
        o = jnp.transpose((o_t[:D, :].reshape(D // 8, 8, B) * inverse[None]).reshape(D, B))
        o32[rows, :] = o
        o_bf[rows, :] = o.astype(BF16)
        column = jnp.transpose(jnp.broadcast_to(inverse[None], (D // 8, 8, B)).reshape(D, B))
        inv_col[rows, :] = column
        q_inv[rows, :] = (q_aug[rows, :D].astype(F32) * (column * score_scale)).astype(BF16)

    def return_tiles(src, out, s):
        dst = out.at[0, :, _rows(me * D, D)]
        local(src.at[mine], dst, rs.at[s])
        remote(src.at[_rows(sib * TOK, TOK)], dst, ss.at[s], rs.at[s], at_seq(sib))

        def one(t, _):
            i = (chip + t) % NB
            ours, other = 2 * i + core, 2 * i + 1 - core
            remote(src.at[_rows(ours * TOK, TOK)], dst, ss.at[s], rs.at[s], at_seq(ours))
            remote(src.at[_rows(other * TOK, TOK)], dst, ss.at[s], rs.at[s], at_seq(other))
            return 0

        lax.fori_loop(1, NB, one, 0)

    return_tiles(o_bf, o_out, S_O)

    drain(g_aug.at[:, pl.ds(0, D)], rs.at[S_G])
    lanes_b = lax.broadcasted_iota(jnp.int32, (B, D), 1)

    for i in range(NB):
        rows = slice(i * B, (i + 1) * B)
        g = g_aug[rows, :D].astype(F32)
        g_inv[rows, :] = (g * inv_col[rows, :]).astype(BF16)
        r = -jnp.sum(o32[rows, :] * g, axis=-1, keepdims=True)
        r1 = r.astype(BF16).astype(F32)
        r2 = (r - r1).astype(BF16).astype(F32)
        r3 = r - r1 - r2
        terms = jnp.where(lanes_b == 0, r1, jnp.where(lanes_b == 1, r2, jnp.where(lanes_b == 2, r3, 0.0)))
        g_aug[rows, D:] = terms.astype(BF16)

    gain_part = jnp.zeros((8, D), F32)
    for j in range(NB):
        rows, queries = slice(j * B, (j + 1) * B), slice(j * B, (_blocks(j)[-1] + 1) * B)
        span = len(_blocks(j)) * B
        v_block = v_aug[rows, :]
        for i in _blocks(j):
            cols = slice((i - j) * B, (i - j + 1) * B)
            gw = lax.dot_general(v_block, g_aug[i * B : (i + 1) * B, :], NT, preferred_element_type=F32)
            ds_keys[j % 2, :, cols] = (e_keys[rows, cols].astype(F32) * gw).astype(BF16)
        ds = ds_keys[j % 2, :, :span]
        dv_buf[rows, :] = _dot(e_keys[rows, :span], g_inv[queries, :])
        dk = _dot(ds, q_inv[queries, :])
        dk_buf[rows, :] = dk
        gain_part = gain_part + _fold(dk * k_aug[rows, :D].astype(F32))
        part_dq = _dot(k_t[:, rows], ds)
        if j == 0:
            dq_acc[:, queries] = part_dq
        else:
            old = slice(queries.start, min(queries.stop, (j + BAND - 1) * B))
            width = old.stop - old.start
            dq_acc[:, old] += part_dq[:, :width]
            if width < span:
                dq_acc[:, old.stop : queries.stop] = part_dq[:, width:]
        theirs = _rows((2 * j + 1 - core) * TOK, TOK)
        slot = pl.ds(j * TOK, TOK)
        remote(dk_buf.at[theirs], x_k.at[slot], ss.at[S_XK], rs_xk.at[j], at_seq(sib))
        remote(dv_buf.at[theirs], x_v.at[slot], ss.at[S_XV], rs_xv.at[j], at_seq(sib))

    part[...] = jnp.sum(gain_part, axis=0, keepdims=True)

    @pl.when(core == 1)
    def _():
        remote(part, pair, ss.at[S_PAIR], rs.at[S_PAIR], at_seq(sib))

    @pl.when(core == 0)
    def _():
        drain(pair, rs.at[S_PAIR])
        part[...] += pair[...]
        pl.semaphore_wait(barrier, DP - 1)

        def send_dp(k, _):
            remote(part, gain_dp.at[pl.ds(dp, 1)], ss.at[S_DP], rs.at[S_DP], at_dp(k))
            return 0

        lax.fori_loop(1, DP, send_dp, 0)
        gain_dp[pl.ds(dp, 1), :] = part[...]

    for i in range(NB):
        rows = slice(i * B, (i + 1) * B)
        inverse_row = inv_row[i * 8 : (i + 1) * 8, :] * score_scale
        dq = jnp.transpose((dq_acc[:, rows].reshape(D // 8, 8, B) * inverse_row[None]).reshape(D, B))
        gq_bf[rows, :] = _norm_backward(dq, q_norm[rows, :], q_unit[rows, :], qg[...]).astype(BF16)
    return_tiles(gq_bf, dq_out, S_DQ)

    for j in range(NB):
        ours, slot = _rows((2 * j + core) * TOK, TOK), pl.ds(j * TOK, TOK)
        drain(x_k.at[slot], rs_xk.at[j])
        drain(x_v.at[slot], rs_xv.at[j])
        gv_bf[slot, :] = (dv_buf[ours, :] + x_v[slot, :]).astype(BF16)
        x = k_buf[ours, :].astype(F32)
        inverse = _inverse_norm(x)
        gk_bf[slot, :] = _norm_backward(dk_buf[ours, :] + x_k[slot, :], inverse, x * inverse, kg[...]).astype(BF16)

    key_cols = _rows(chip * D, D)
    dk_dst, dv_dst = dk_out.at[0, :, key_cols], dv_out.at[0, :, key_cols]
    local(gk_bf.at[_rows(chip * TOK, TOK)], dk_dst, rs.at[S_DK])
    local(gv_bf.at[_rows(chip * TOK, TOK)], dv_dst, rs.at[S_DV])

    def return_keys(t, _):
        j = (chip + t) % NB
        slot = _rows(j * TOK, TOK)
        remote(gk_bf.at[slot], dk_dst, ss.at[S_DK], rs.at[S_DK], at_seq(2 * j + core))
        remote(gv_bf.at[slot], dv_dst, ss.at[S_DV], rs.at[S_DV], at_seq(2 * j + core))
        return 0

    lax.fori_loop(1, NB, return_keys, 0)

    @pl.when(core == 0)
    def _():
        drain(gain_dp.at[pl.ds(0, DP - 1)], rs.at[S_DP])
        gain_sum[...] = jnp.sum(gain_dp[...], axis=0, keepdims=True)

        def send_gain(k, _):
            remote(gain_sum, gain_seq.at[pl.ds(chip, 1)], ss.at[S_GAIN], rs.at[S_GAIN], at_seq((me + k) % SEQ))
            return 0

        lax.fori_loop(1, SEQ, send_gain, 0)
        gain_seq[pl.ds(chip, 1), :] = gain_sum[...]

    drain(o_out.at[0], rs.at[S_O])
    drain(dq_out.at[0], rs.at[S_DQ])
    drain(dk_out.at[0], rs.at[S_DK])
    drain(dv_out.at[0], rs.at[S_DV])

    @pl.when(core == 0)
    def _():
        drain(gain_seq.at[pl.ds(0, NB - 1)], rs.at[S_GAIN])

    @pl.when(core == 1)
    def _():
        drain(gain_seq, rs.at[S_GAIN])

    total = jnp.sum(gain_seq[...], axis=0, keepdims=True)
    gain_out[0:1, :] = total / qg[...]
    gain_out[1:2, :] = total / kg[...]
    most, some = pl.ds(0, LEN - TOK), pl.ds(0, LEN // 2 - TOK)
    drain(seg_buf.at[pl.ds(0, SEQ - 1)], ss.at[S_SEG])
    drain(k_buf.at[some], ss.at[S_K])
    drain(q_buf.at[most], ss.at[S_Q])
    drain(k_buf.at[some], ss.at[S_V])
    drain(q_buf.at[most], ss.at[S_G])
    drain(k_buf.at[half], ss.at[S_KF])
    drain(k_buf.at[half], ss.at[S_VF])
    drain(o_bf.at[most], ss.at[S_O])
    drain(gq_bf.at[most], ss.at[S_DQ])
    drain(x_k, ss.at[S_XK])
    drain(x_v, ss.at[S_XV])
    drain(gk_bf.at[some], ss.at[S_DK])
    drain(gv_bf.at[some], ss.at[S_DV])

    @pl.when(core == 1)
    def _():
        drain(part, ss.at[S_PAIR])

    @pl.when(core == 0)
    def _():
        drain(gain_dp.at[pl.ds(0, DP - 1)], ss.at[S_DP])
        drain(gain_dp.at[pl.ds(0, SEQ - 1)], ss.at[S_GAIN])


def finish(o_in, dq_in, dk_in, dv_in, gains, o_out, dq_out, dk_out, dv_out, q_out, k_out, *, q_scale, k_scale):
    for src, dst in ((o_in, o_out), (dq_in, dq_out), (dk_in, dk_out), (dv_in, dv_out)):
        dst[...] = src[...]
    q_out[...] = gains[0:1, :] * q_scale
    k_out[...] = gains[1:2, :] * k_scale


def shards(q_raw, key_unnormed, value_input, grad_attended, segment_ids, q_gain, key_norm_gain):
    hbm = pl.BlockSpec(memory_space=pltpu.HBM)
    anywhere = pl.BlockSpec(memory_space=pl.ANY)
    vmem = pl.BlockSpec(memory_space=pltpu.VMEM)
    q_heads, kv_heads = q_raw.shape[2] // D, key_unnormed.shape[2] // D
    dma = pltpu.SemaphoreType.DMA
    results = [
        jax.ShapeDtypeStruct(q_raw.shape, BF16),
        jax.ShapeDtypeStruct(q_raw.shape, BF16),
        jax.ShapeDtypeStruct(key_unnormed.shape, BF16),
        jax.ShapeDtypeStruct(key_unnormed.shape, BF16),
    ]
    staged = pl.pallas_call(
        kernel,
        out_shape=results + [jax.ShapeDtypeStruct((8, D), F32)],
        in_specs=[hbm] * 7,
        out_specs=[anywhere] * 4 + [vmem],
        scratch_shapes=[
            pltpu.VMEM((LEN, D), BF16),
            pltpu.VMEM((LEN, D), BF16),
            pltpu.VMEM((LEN, 2 * D), BF16),
            pltpu.VMEM((LEN, 2 * D), BF16),
            pltpu.VMEM((SEQ, TOK), jnp.int32),
            pltpu.VMEM((LEN, 2 * D), BF16),
            pltpu.VMEM((LEN, 2 * D), BF16),
            pltpu.VMEM((D, LEN), BF16),
            pltpu.VMEM((D + ONES, LEN), BF16),
            pltpu.VMEM((LEN, BAND * B), BF16),
            pltpu.VMEM((NB * BAND * B, B), BF16),
            pltpu.VMEM((2, B, BAND * B), BF16),
            pltpu.VMEM((LEN, D), F32),
            pltpu.VMEM((LEN, D), F32),
            pltpu.VMEM((LEN, D), F32),
            pltpu.VMEM((LEN, D), BF16),
            pltpu.VMEM((LEN, D), F32),
            pltpu.VMEM((NB * 8, B), F32),
            pltpu.VMEM((LEN, D), BF16),
            pltpu.VMEM((LEN, D), BF16),
            pltpu.VMEM((D, LEN), F32),
            pltpu.VMEM((LEN, D), F32),
            pltpu.VMEM((LEN, D), F32),
            pltpu.VMEM((LEN // 2, D), F32),
            pltpu.VMEM((LEN // 2, D), F32),
            pltpu.VMEM((LEN, D), BF16),
            pltpu.VMEM((LEN // 2, D), BF16),
            pltpu.VMEM((LEN // 2, D), BF16),
            pltpu.VMEM((1, D), F32),
            pltpu.VMEM((1, D), F32),
            pltpu.VMEM((1, D), F32),
            pltpu.VMEM((1, D), F32),
            pltpu.VMEM((DP, D), F32),
            pltpu.VMEM((1, D), F32),
            pltpu.VMEM((NB, D), F32),
            dma((18,)),
            dma((18,)),
            dma((8,)),
            dma((8,)),
            dma((8,)),
            dma((8,)),
            pltpu.SemaphoreType.REGULAR,
        ],
        compiler_params=pltpu.CompilerParams(
            collective_id=0, has_side_effects=True, vmem_limit_bytes=60 << 20
        ),
        name="attention",
    )(
        q_raw,
        key_unnormed,
        value_input,
        grad_attended,
        segment_ids,
        q_gain.reshape(1, D),
        key_norm_gain.reshape(1, D),
    )
    tokens = lax.axis_size("dp") * lax.axis_size("seq") * q_raw.shape[1]
    row = jax.ShapeDtypeStruct((1, D), F32)
    tiles = [pl.BlockSpec((1, TOK // STEPS, r.shape[2]), lambda t: (0, t, 0)) for r in results]
    rows = [pl.BlockSpec((count, D), lambda t: (0, 0)) for count in (8, 1, 1)]
    *tiles, grad_q_gain, key_gain_gradient = pl.pallas_call(
        functools.partial(finish, q_scale=(tokens * q_heads) ** -0.5, k_scale=(tokens * kv_heads) ** -0.5),
        out_shape=results + [row, row],
        grid=(STEPS,),
        in_specs=tiles + rows[:1],
        out_specs=tiles + rows[1:],
        name="finish",
    )(*staged)
    return *tiles, grad_q_gain.reshape(D), key_gain_gradient.reshape(D)


def solution(mesh):
    tokens = P("dp", "seq", None)
    in_specs = (tokens, tokens, tokens, tokens, P("dp", "seq"), P(), P())
    out_specs = (tokens, tokens, tokens, tokens, P(), P())
    return jax.shard_map(shards, mesh=mesh, in_specs=in_specs, out_specs=out_specs, check_vma=False)
```

```python
import functools
import math

import jax
import jax.numpy as jnp
from jax import lax
from jax.experimental import pallas as pl
from jax.experimental.pallas import tpu as pltpu
from jax.sharding import PartitionSpec as P

MESH = pl.DeviceIdType.MESH
EPSILON = 1e-06
D = 128
TOK = 128
SEQ = 16
DP = 32
HEADS_KV = 8
LEN = TOK * SEQ
B = 256
NB = LEN // B
STEPS = 2
BAND = 5
ONES = 16
FAR = -16384.0
F32, BF16 = jnp.float32, jnp.bfloat16
NT = (((1,), (1,)), ((), ()))


def _rows(start, count):
    return pl.ds(pl.multiple_of(start, count), count)


def _dot(a, b):
    return jnp.dot(a, b, preferred_element_type=F32)


def _inverse_norm(x):
    return lax.rsqrt(jnp.mean(x * x, axis=-1, keepdims=True) + EPSILON)


def _norm_backward(grad, inverse, unit, gain):
    scaled = grad * gain
    return inverse * (scaled - unit * jnp.mean(scaled * unit, axis=-1, keepdims=True))


def _fold(x):
    return jnp.sum(x.reshape(x.shape[0] // 8, 8, D), axis=0)


def _blocks(j):
    return range(j, min(j + BAND, NB))


def _first_key(i):
    return max(0, i - BAND + 1)


def kernel(
    q_in, k_in, v_in, g_in, seg_in, qg_in, kg_in,
    o_out, dq_out, dk_out, dv_out, gain_out,
    q_buf, k_buf, v_aug, g_aug, seg_buf, q_aug, k_aug, k_t, v_t, e_keys, e_queries, ds_keys, ds_queries, q_unit, q_norm,
    o32, o_bf, inv_col, inv_row, g_inv, q_inv, dk_buf, dv_buf, x_k, x_v,
    gq_bf, gk_bf, gv_bf, qg, kg, part, gain_seq, gain_sum, gain_dp,
    ss, rs, rs_k, rs_v, rs_xk, rs_xv, opened,
):
    dp, me = lax.axis_index("dp"), lax.axis_index("seq")
    chip, core = me // 2, me % 2
    sib = me + 1 - 2 * core
    score_scale = D ** (-0.5)
    exponent_scale = score_scale * math.log2(math.e)

    (S_SEG, S_K, S_Q, S_V, S_G, S_KF, S_VF, S_O, S_DQ, S_XK, S_XV, S_DK, S_DV, S_DP, S_GAIN, S_QG, S_KG) = range(17)

    def at_seq(i):
        return (dp, i)

    def at_dp(flip, k):
        return (((dp // 16 + flip) % 2) * 16 + (dp + k) % 16, me)

    def far_first(act):
        def both(n, _):
            k = 8 + ((n + 1) // 2) * (2 * (n % 2) - 1)
            act(at_dp(0, k))
            act(at_dp(1, k))
            return 0

        lax.fori_loop(0, 15, both, 0)
        act(at_dp(1, 0))

    barrier = pltpu.get_barrier_semaphore()

    def greet(k, _):
        to = 2 * ((chip + k) % NB) + 1

        @pl.when(to != me)
        def _():
            pl.semaphore_signal(barrier, inc=1, device_id=at_seq(to), device_id_type=MESH)

        return 0

    lax.fori_loop(0, NB, greet, 0)

    lane = lax.broadcasted_iota(jnp.int32, (D, D), 1)
    v_aug[:, D:] = jnp.ones((LEN, D), BF16)
    v_t[D:, :] = jnp.ones((ONES, LEN), BF16)
    pltpu.make_async_copy(qg_in, qg, rs.at[S_QG]).start()
    pltpu.make_async_copy(kg_in, kg, rs.at[S_KG]).start()

    @pl.when(core == 1)
    def _():
        pl.semaphore_wait(barrier, SEQ - 1)
        pl.semaphore_signal(opened, inc=1, device_id=at_seq(sib), device_id_type=MESH)

    @pl.when(core == 0)
    def _():
        pl.semaphore_wait(opened, 1)


    def remote(src, dst, send, recv, peer):
        pltpu.make_async_remote_copy(src_ref=src, dst_ref=dst, send_sem=send, recv_sem=recv, device_id=peer, device_id_type=MESH).start()

    def local(src, dst, sem):
        pltpu.make_async_copy(src, dst, sem).start()

    def drain(ref, sem):
        pltpu.make_async_copy(ref, ref, sem).wait()

    mine = _rows(me * TOK, TOK)

    def send_seg(k, _):
        remote(seg_in, seg_buf.at[pl.ds(me, 1)], ss.at[S_SEG], rs.at[S_SEG], at_seq((me + k) % SEQ))
        return 0

    local(seg_in, seg_buf.at[pl.ds(me, 1)], rs.at[S_SEG])
    lax.fori_loop(1, SEQ, send_seg, 0)

    def send_heads(src, dst, s):
        local(src.at[0, :, _rows(me * D, D)], dst, rs.at[s])

        def one(k, _):
            to = (me + k) % SEQ
            remote(src.at[0, :, _rows(to * D, D)], dst, ss.at[s], rs.at[s], at_seq(to))
            return 0

        lax.fori_loop(1, SEQ, one, 0)

    def send_key_heads(src, dst, s, sems):
        local(src.at[0, :, _rows(chip * D, D)], dst, sems.at[chip])

        def one(k, _):
            to = (me + 2 * k) % SEQ
            remote(src.at[0, :, _rows((to // 2) * D, D)], dst, ss.at[s], sems.at[chip], at_seq(to))
            return 0

        lax.fori_loop(1, SEQ // 2, one, 0)

    send_key_heads(k_in, k_buf.at[mine], S_K, rs_k)
    send_key_heads(v_in, v_aug.at[mine, pl.ds(0, D)], S_V, rs_v)
    send_heads(q_in, q_buf.at[mine], S_Q)
    send_heads(g_in, g_aug.at[mine, pl.ds(0, D)], S_G)

    @pl.when(core == 0)
    def _():
        far_first(lambda peer: pl.semaphore_signal(barrier, inc=1, device_id=peer, device_id_type=MESH))

    drain(qg, rs.at[S_QG])
    drain(kg, rs.at[S_KG])
    drain(seg_buf, rs.at[S_SEG])

    def documents(i, _):
        ids = seg_buf[pl.ds(i, 1), :].astype(F32)
        column = jnp.transpose(jnp.broadcast_to(ids, (D, D)))
        same = column == lane.astype(F32)
        rows = _rows(i * TOK, TOK)
        q_aug[rows, D:] = jnp.where(same, 1.0, 0.0).astype(BF16)
        k_aug[rows, D:] = jnp.where(same | (lane > 3), 0.0, FAR).astype(BF16)
        return 0

    lax.fori_loop(0, SEQ, documents, 0, unroll=4)

    def forward(k, sems, s, view):
        owner = (me - 2 * k + SEQ) % SEQ
        ref = view(_rows(owner * TOK, TOK))
        drain(ref, sems.at[owner // 2])
        remote(ref, ref, ss.at[s], rs.at[s], at_seq(sib))

    def forward_key(k, _):
        forward(k, rs_k, S_KF, lambda rows: k_buf.at[rows])
        return 0

    lax.fori_loop(0, SEQ // 2, forward_key, 0)
    half = pl.ds(0, LEN // 2)
    drain(k_buf.at[half], rs.at[S_KF])

    def norm_keys(i, _):
        rows = _rows(i * B, B)
        x = k_buf[rows, :].astype(F32)
        scaled = (x * _inverse_norm(x) * kg[...]).astype(BF16)
        k_aug[rows, :D] = scaled
        k_t[:, rows] = jnp.transpose(scaled)
        return 0

    lax.fori_loop(0, NB, norm_keys, 0, unroll=4)

    def forward_value(k, _):
        forward(k, rs_v, S_VF, lambda rows: v_aug.at[rows, pl.ds(0, D)])
        return 0

    lax.fori_loop(0, SEQ // 2, forward_value, 0)
    drain(v_aug.at[half, pl.ds(0, D)], rs.at[S_VF])

    def transpose_values(i, _):
        rows = _rows(i * B, B)
        v_t[:D, rows] = jnp.transpose(v_aug[rows, :D])
        return 0

    lax.fori_loop(0, NB, transpose_values, 0, unroll=4)

    drain(q_buf, rs.at[S_Q])

    def norm_queries(i, _):
        rows = _rows(i * B, B)
        x = q_buf[rows, :].astype(F32)
        inverse = _inverse_norm(x)
        unit = x * inverse
        q_norm[rows, :] = jnp.broadcast_to(inverse, (B, D))
        q_unit[rows, :] = unit
        q_aug[rows, :D] = (unit * qg[...]).astype(BF16)
        return 0

    lax.fori_loop(0, NB, norm_queries, 0, unroll=4)
    causal = lax.broadcasted_iota(jnp.int32, (B, B), 0) <= lax.broadcasted_iota(jnp.int32, (B, B), 1)

    for j in range(NB):
        k_block = k_aug[j * B : (j + 1) * B, :]
        for i in _blocks(j):
            s = lax.dot_general(k_block, q_aug[i * B : (i + 1) * B, :], NT, preferred_element_type=F32)
            e = jnp.exp2(s * exponent_scale)
            if i == j:
                e = jnp.where(causal, e, 0.0)
            e = e.astype(BF16)
            e_keys[j * B : (j + 1) * B, (i - j) * B : (i - j + 1) * B] = e
            at = (i * BAND + j - _first_key(i)) * B
            e_queries[at : at + B, :] = e

    for i in range(NB):
        first, rows = _first_key(i), slice(i * B, (i + 1) * B)
        keys = (i + 1 - first) * B
        o_t = _dot(v_t[:, first * B : (i + 1) * B], e_queries[i * BAND * B : i * BAND * B + keys, :])
        inverse = 1.0 / o_t[D : D + 8, :]
        inv_row[i * 8 : (i + 1) * 8, :] = inverse
        o = jnp.transpose((o_t[:D, :].reshape(D // 8, 8, B) * inverse[None]).reshape(D, B))
        o32[rows, :] = o
        o_bf[rows, :] = o.astype(BF16)
        column = jnp.transpose(jnp.broadcast_to(inverse[None], (D // 8, 8, B)).reshape(D, B))
        inv_col[rows, :] = column
        q_inv[rows, :] = (q_aug[rows, :D].astype(F32) * (column * score_scale)).astype(BF16)

    def return_tiles(src, out, s):
        dst = out.at[0, :, _rows(me * D, D)]
        local(src.at[mine], dst, rs.at[s])
        remote(src.at[_rows(sib * TOK, TOK)], dst, ss.at[s], rs.at[s], at_seq(sib))

        def one(t, _):
            i = (chip + t) % NB
            ours, other = 2 * i + core, 2 * i + 1 - core
            remote(src.at[_rows(ours * TOK, TOK)], dst, ss.at[s], rs.at[s], at_seq(ours))
            remote(src.at[_rows(other * TOK, TOK)], dst, ss.at[s], rs.at[s], at_seq(other))
            return 0

        lax.fori_loop(1, NB, one, 0)

    return_tiles(o_bf, o_out, S_O)

    drain(g_aug.at[:, pl.ds(0, D)], rs.at[S_G])
    lanes_b = lax.broadcasted_iota(jnp.int32, (B, D), 1)

    for i in range(NB):
        rows = slice(i * B, (i + 1) * B)
        g = g_aug[rows, :D].astype(F32)
        g_inv[rows, :] = (g * inv_col[rows, :]).astype(BF16)
        r = -jnp.sum(o32[rows, :] * g, axis=-1, keepdims=True)
        r1 = r.astype(BF16).astype(F32)
        r2 = (r - r1).astype(BF16).astype(F32)
        r3 = r - r1 - r2
        terms = jnp.where(lanes_b == 0, r1, jnp.where(lanes_b == 1, r2, jnp.where(lanes_b == 2, r3, 0.0)))
        g_aug[rows, D:] = terms.astype(BF16)

    def exchange(j, src, dst, s, sems):
        theirs = _rows((2 * j + 1 - core) * TOK, TOK)
        remote(src.at[theirs], dst.at[pl.ds(j * TOK, TOK)], ss.at[s], sems.at[j], at_seq(sib))

    gain_part = jnp.zeros((8, D), F32)
    for j in range(NB):
        rows, queries = slice(j * B, (j + 1) * B), slice(j * B, (_blocks(j)[-1] + 1) * B)
        v_block = v_aug[rows, :]
        for i in _blocks(j):
            cols = slice((i - j) * B, (i - j + 1) * B)
            gw = lax.dot_general(v_block, g_aug[i * B : (i + 1) * B, :], NT, preferred_element_type=F32)
            ds = (e_keys[rows, cols].astype(F32) * gw).astype(BF16)
            ds_keys[j % 2, :, cols] = ds
            at = (i * BAND + j - _first_key(i)) * B
            ds_queries[at : at + B, :] = ds
        dk = _dot(ds_keys[j % 2, :, : queries.stop - queries.start], q_inv[queries, :])
        dk_buf[rows, :] = dk
        gain_part = gain_part + _fold(dk * k_aug[rows, :D].astype(F32))
        exchange(j, dk_buf, x_k, S_XK, rs_xk)

    part[...] = jnp.sum(gain_part, axis=0, keepdims=True)

    def send_gain(k, _):
        remote(part, gain_seq.at[pl.ds(me, 1)], ss.at[S_GAIN], rs.at[S_GAIN], at_seq((me + k) % SEQ))
        return 0

    lax.fori_loop(1, SEQ, send_gain, 0)
    gain_seq[pl.ds(me, 1), :] = part[...]

    def return_keys(src, out, s):
        dst = out.at[0, :, _rows(chip * D, D)]
        local(src.at[_rows(chip * TOK, TOK)], dst, rs.at[s])

        def one(t, _):
            j = (chip + t) % NB
            remote(src.at[_rows(j * TOK, TOK)], dst, ss.at[s], rs.at[s], at_seq(2 * j + core))
            return 0

        lax.fori_loop(1, NB, one, 0)

    for j in range(NB):
        ours, slot = _rows((2 * j + core) * TOK, TOK), pl.ds(j * TOK, TOK)
        drain(x_k.at[slot], rs_xk.at[j])
        x = k_buf[ours, :].astype(F32)
        inverse = _inverse_norm(x)
        gk_bf[slot, :] = _norm_backward(dk_buf[ours, :] + x_k[slot, :], inverse, x * inverse, kg[...]).astype(BF16)

    return_keys(gk_bf, dk_out, S_DK)

    for i in range(NB):
        first, rows = _first_key(i), slice(i * B, (i + 1) * B)
        keys = (i + 1 - first) * B
        dq_t = _dot(k_t[:, first * B : (i + 1) * B], ds_queries[i * BAND * B : i * BAND * B + keys, :])
        inverse_row = inv_row[i * 8 : (i + 1) * 8, :] * score_scale
        dq = jnp.transpose((dq_t.reshape(D // 8, 8, B) * inverse_row[None]).reshape(D, B))
        gq_bf[rows, :] = _norm_backward(dq, q_norm[rows, :], q_unit[rows, :], qg[...]).astype(BF16)
    return_tiles(gq_bf, dq_out, S_DQ)

    drain(gain_seq.at[pl.ds(0, SEQ - 1)], rs.at[S_GAIN])
    gain_sum[...] = jnp.sum(gain_seq[...], axis=0, keepdims=True)

    @pl.when(core == 0)
    def _():
        pl.semaphore_wait(barrier, DP - 1)
        pl.semaphore_signal(opened, inc=1, device_id=at_seq(sib), device_id_type=MESH)

    @pl.when(core == 1)
    def _():
        pl.semaphore_wait(opened, 1)

    far_first(lambda peer: remote(gain_sum, gain_dp.at[pl.ds(dp, 1)], ss.at[S_DP], rs.at[S_DP], peer))
    gain_dp[pl.ds(dp, 1), :] = gain_sum[...]
    for j in range(NB):
        rows, queries = slice(j * B, (j + 1) * B), slice(j * B, (_blocks(j)[-1] + 1) * B)
        dv_buf[rows, :] = _dot(e_keys[rows, : queries.stop - queries.start], g_inv[queries, :])
        exchange(j, dv_buf, x_v, S_XV, rs_xv)


    for j in range(NB):
        ours, slot = _rows((2 * j + core) * TOK, TOK), pl.ds(j * TOK, TOK)
        drain(x_v.at[slot], rs_xv.at[j])
        gv_bf[slot, :] = (dv_buf[ours, :] + x_v[slot, :]).astype(BF16)

    return_keys(gv_bf, dv_out, S_DV)

    drain(o_out.at[0], rs.at[S_O])
    drain(dq_out.at[0], rs.at[S_DQ])
    drain(dk_out.at[0], rs.at[S_DK])
    drain(dv_out.at[0], rs.at[S_DV])

    most, some = pl.ds(0, LEN - TOK), pl.ds(0, LEN // 2 - TOK)
    drain(seg_buf.at[pl.ds(0, SEQ - 1)], ss.at[S_SEG])
    drain(k_buf.at[some], ss.at[S_K])
    drain(q_buf.at[most], ss.at[S_Q])
    drain(k_buf.at[some], ss.at[S_V])
    drain(q_buf.at[most], ss.at[S_G])
    drain(k_buf.at[half], ss.at[S_KF])
    drain(k_buf.at[half], ss.at[S_VF])
    drain(o_bf.at[most], ss.at[S_O])
    drain(gq_bf.at[most], ss.at[S_DQ])
    drain(x_k, ss.at[S_XK])
    drain(x_v, ss.at[S_XV])
    drain(gk_bf.at[some], ss.at[S_DK])
    drain(gv_bf.at[some], ss.at[S_DV])

    drain(gain_dp.at[pl.ds(0, DP - 1)], ss.at[S_DP])
    drain(gain_seq.at[pl.ds(0, SEQ - 1)], ss.at[S_GAIN])

    drain(gain_dp.at[pl.ds(0, DP - 1)], rs.at[S_DP])
    total = jnp.sum(gain_dp[...], axis=0, keepdims=True)
    gain_out[0:1, :] = total / qg[...]
    gain_out[1:2, :] = total / kg[...]


def finish(o_in, dq_in, dk_in, dv_in, gains, o_out, dq_out, dk_out, dv_out, q_out, k_out, *, q_scale, k_scale):
    for src, dst in ((o_in, o_out), (dq_in, dq_out), (dk_in, dk_out), (dv_in, dv_out)):
        dst[...] = src[...]
    q_out[...] = gains[0:1, :] * q_scale
    k_out[...] = gains[1:2, :] * k_scale


def shards(q_raw, key_unnormed, value_input, grad_attended, segment_ids, q_gain, key_norm_gain):
    hbm = pl.BlockSpec(memory_space=pltpu.HBM)
    anywhere = pl.BlockSpec(memory_space=pl.ANY)
    vmem = pl.BlockSpec(memory_space=pltpu.VMEM)
    q_heads, kv_heads = q_raw.shape[2] // D, key_unnormed.shape[2] // D
    dma = pltpu.SemaphoreType.DMA
    results = [
        jax.ShapeDtypeStruct(q_raw.shape, BF16),
        jax.ShapeDtypeStruct(q_raw.shape, BF16),
        jax.ShapeDtypeStruct(key_unnormed.shape, BF16),
        jax.ShapeDtypeStruct(key_unnormed.shape, BF16),
    ]
    staged = pl.pallas_call(
        kernel,
        out_shape=results + [jax.ShapeDtypeStruct((8, D), F32)],
        in_specs=[hbm] * 7,
        out_specs=[anywhere] * 4 + [vmem],
        scratch_shapes=[
            pltpu.VMEM((LEN, D), BF16),
            pltpu.VMEM((LEN, D), BF16),
            pltpu.VMEM((LEN, 2 * D), BF16),
            pltpu.VMEM((LEN, 2 * D), BF16),
            pltpu.VMEM((SEQ, TOK), jnp.int32),
            pltpu.VMEM((LEN, 2 * D), BF16),
            pltpu.VMEM((LEN, 2 * D), BF16),
            pltpu.VMEM((D, LEN), BF16),
            pltpu.VMEM((D + ONES, LEN), BF16),
            pltpu.VMEM((LEN, BAND * B), BF16),
            pltpu.VMEM((NB * BAND * B, B), BF16),
            pltpu.VMEM((2, B, BAND * B), BF16),
            pltpu.VMEM((NB * BAND * B, B), BF16),
            pltpu.VMEM((LEN, D), F32),
            pltpu.VMEM((LEN, D), F32),
            pltpu.VMEM((LEN, D), F32),
            pltpu.VMEM((LEN, D), BF16),
            pltpu.VMEM((LEN, D), F32),
            pltpu.VMEM((NB * 8, B), F32),
            pltpu.VMEM((LEN, D), BF16),
            pltpu.VMEM((LEN, D), BF16),
            pltpu.VMEM((LEN, D), F32),
            pltpu.VMEM((LEN, D), F32),
            pltpu.VMEM((LEN // 2, D), F32),
            pltpu.VMEM((LEN // 2, D), F32),
            pltpu.VMEM((LEN, D), BF16),
            pltpu.VMEM((LEN // 2, D), BF16),
            pltpu.VMEM((LEN // 2, D), BF16),
            pltpu.VMEM((1, D), F32),
            pltpu.VMEM((1, D), F32),
            pltpu.VMEM((1, D), F32),
            pltpu.VMEM((SEQ, D), F32),
            pltpu.VMEM((1, D), F32),
            pltpu.VMEM((DP, D), F32),
            dma((17,)),
            dma((17,)),
            dma((8,)),
            dma((8,)),
            dma((8,)),
            dma((8,)),
            pltpu.SemaphoreType.REGULAR,
        ],
        compiler_params=pltpu.CompilerParams(
            collective_id=0, has_side_effects=True, vmem_limit_bytes=60 << 20
        ),
        name="attention",
    )(
        q_raw,
        key_unnormed,
        value_input,
        grad_attended,
        segment_ids,
        q_gain.reshape(1, D),
        key_norm_gain.reshape(1, D),
    )
    tokens = lax.axis_size("dp") * lax.axis_size("seq") * q_raw.shape[1]
    row = jax.ShapeDtypeStruct((1, D), F32)
    tiles = [pl.BlockSpec((1, TOK // STEPS, r.shape[2]), lambda t: (0, t, 0)) for r in results]
    rows = [pl.BlockSpec((count, D), lambda t: (0, 0)) for count in (8, 1, 1)]
    *tiles, grad_q_gain, key_gain_gradient = pl.pallas_call(
        functools.partial(finish, q_scale=(tokens * q_heads) ** -0.5, k_scale=(tokens * kv_heads) ** -0.5),
        out_shape=results + [row, row],
        grid=(STEPS,),
        in_specs=tiles + rows[:1],
        out_specs=tiles + rows[1:],
        name="finish",
    )(*staged)
    return *tiles, grad_q_gain.reshape(D), key_gain_gradient.reshape(D)


def solution(mesh):
    tokens = P("dp", "seq", None)
    in_specs = (tokens, tokens, tokens, tokens, P("dp", "seq"), P(), P())
    out_specs = (tokens, tokens, tokens, tokens, P(), P())
    return jax.shard_map(shards, mesh=mesh, in_specs=in_specs, out_specs=out_specs, check_vma=False)
```
